128 devices in a mesh: seq: 32 (over y, x, core), head: 4 (over z), dp: 1.
Axes of the slice: x: 4, y: 4, z: 4, core: 2. Of those that a mesh axis runs over, the one named last changes fastest.
Arguments:
- token_ids: int32 [8192], P(('dp', 'seq')), may hold values from 0 to 8191, as said below
- token_tables: bfloat16 [2, 256, 8192], P(None, 'head'), may hold values from -12 to 1, as said below
- ssm_input: bfloat16 [8192, 16384], P(('dp', 'seq'), 'head'), may hold values from -6 to 6
- ssm_gate: bfloat16 [8192, 16384], P(('dp', 'seq'), 'head'), may hold values from -6 to 6
- ssm_bc: bfloat16 [8192, 2, 2048], P(('dp', 'seq'), None, 'head'), may hold values from -6 to 6
- conv_input: bfloat16 [4, 16384], P(None, 'head'), may hold values from -3 to 3
- conv_bc: bfloat16 [4, 2, 2048], P(None, None, 'head'), may hold values from -3 to 3
- skip_gain: float32 [256], P('head'), may hold values from 0.5 to 1.5
- norm_gain: bfloat16 [16384], P('head'), may hold values from 0.25 to 1.75
- queries: bfloat16 [8192, 8192], P(('dp', 'seq'), 'head'), may hold values from -24 to 24
- keys_values: bfloat16 [8192, 2, 1024], P(('dp', 'seq'), None, 'head'), may hold values from -9 to 9
Outputs:
- mamba_out: bfloat16 [8192, 16384], P(('dp', 'seq'), 'head')
- attn_out: bfloat16 [8192, 8192], P(('dp', 'seq'), 'head')
The draws below stay inside these ranges and needn't reach their ends.
Inputs may be any that keep to these rules, and one draw needn't show every extreme that they name: `token_ids`: token ids into the tables. `token_tables`: slice 0 holds positive decay rates.
All inputs are finite; a program needn't handle non-finite values.
Results may differ from the reference program's by a relative error of at most 0.0065.
Values may be sent and summed in bfloat16 or wider, within the bound.
No kernel may reach another device: no remote copies, remote signals or barrier semaphores. Data moves between devices by JAX's collectives and lax.ppermute only.
A program may use at most 384 MiB of HBM per device.

```python
import jax
import jax.numpy as jnp
from jax import lax

MIXER_HEADS = 256
MHDIM = 64
STATE = 256
GROUPS = 8
CONV = 4
QHEADS = 64
KVHEADS = 8
HDIM = 128
VOCABULARY_SIZE = 8192
SPAN = 128
TOKENS = 8192


def head_rates(key, slow_share):
    picks = jax.random.uniform(jax.random.fold_in(key, 21), (MIXER_HEADS,))
    slower = jax.random.uniform(jax.random.fold_in(key, 22), (MIXER_HEADS,), minval=jnp.log(0.1 / TOKENS), maxval=jnp.log(1.0 / TOKENS))
    faster = jax.random.uniform(jax.random.fold_in(key, 23), (MIXER_HEADS,), minval=jnp.log(1.0 / TOKENS), maxval=jnp.log(0.05))
    return jnp.exp(jnp.where(picks < slow_share, slower, faster))


def draw_token_ids(key, part):
    key = jax.random.fold_in(key, 1)
    return jax.random.randint(jax.random.fold_in(key, 1), (TOKENS,), 0, VOCABULARY_SIZE).astype(jnp.int32)


def draw_token_tables(key, part):
    key = jax.random.fold_in(key, 2)
    rate_values = head_rates(key, 0.5)
    coarse_rate = jax.random.uniform(jax.random.fold_in(key, 31), (MIXER_HEADS, VOCABULARY_SIZE), minval=0.5, maxval=2.0)
    rough_step = jax.random.uniform(jax.random.fold_in(key, 32), (MIXER_HEADS, VOCABULARY_SIZE), minval=0.5, maxval=2.0)
    flagged_entries = jax.random.uniform(jax.random.fold_in(key, 34), (VOCABULARY_SIZE,)) < 8.0 / TOKENS
    sudden_rate = jax.random.uniform(jax.random.fold_in(key, 33), (MIXER_HEADS, VOCABULARY_SIZE), minval=0.2, maxval=0.7)
    decay_rate_row = jnp.where(flagged_entries[None, :], sudden_rate, rate_values[:, None] * coarse_rate)
    step_size = jnp.sqrt(rate_values)[:, None] * rough_step
    step_row = jnp.log(jnp.expm1(step_size))
    return jnp.stack([decay_rate_row, step_row]).astype(jnp.bfloat16)


def draw_queries(key, part):
    key = jax.random.fold_in(key, 3)
    base = 2.5 * jnp.clip(jax.random.normal(key, (TOKENS, QHEADS * HDIM)), -6.0, 6.0)
    return base.astype(jnp.bfloat16)


def draw_keys_values(key, part):
    key = jax.random.fold_in(key, 4)
    base = jnp.clip(jax.random.normal(key, (TOKENS, 2, KVHEADS * HDIM)), -6.0, 6.0)
    return base.astype(jnp.bfloat16)


def level_of(own_key, dims, pieces, least, top_value):
    gain, own = 1.0, jax.random.fold_in(own_key, 6)
    for position, parts in pieces:
        heights = jnp.exp(jax.random.uniform(jax.random.fold_in(own, position), (parts,), jnp.float32, least / len(pieces), top_value / len(pieces)))
        gain = gain * jnp.repeat(heights, dims[position] // parts).reshape([-1 if axis == position else 1 for axis in range(len(dims))])
    return gain


def bell_draw(stream_key, shape, width, limit, cuts=(), held_as=jnp.bfloat16):
    result = width * jax.random.normal(stream_key, shape, jnp.float32)
    if cuts:
        result = result * level_of(stream_key, shape, cuts, -0.22, 0.18)
    return jnp.clip(result, -limit, limit).astype(held_as)


def setup_inputs(seed: int = 0, part: int = 0) -> dict:
    streams_of = jax.random.split(jax.random.key(seed), 12)
    part_splits = jax.random.split(jax.random.fold_in(streams_of[11], part), 12)
    token_ids = draw_token_ids(jax.random.fold_in(jax.random.fold_in(streams_of[11], part), 71), part)
    token_tables = draw_token_tables(jax.random.fold_in(streams_of[11], 71), part)
    ssm_input = bell_draw(part_splits[2], (TOKENS, MIXER_HEADS * MHDIM), 1.0, 6.0, ((0, 32), (1, 4)))
    ssm_gate = bell_draw(part_splits[3], (TOKENS, MIXER_HEADS * MHDIM), 1.0, 6.0, ((0, 32), (1, 4)))
    ssm_bc = bell_draw(part_splits[4], (TOKENS, 2, GROUPS * STATE), 1.0, 6.0, ((0, 32), (2, 4)))
    conv_input = bell_draw(streams_of[5], (CONV, MIXER_HEADS * MHDIM), CONV ** -0.5, 3.0, ((1, 4),))
    conv_bc = bell_draw(streams_of[6], (CONV, 2, GROUPS * STATE), CONV ** -0.5, 3.0, ((2, 4),))
    skip_gain = jnp.clip(0.5 + 1.0 * jax.random.uniform(streams_of[7], (MIXER_HEADS,), jnp.float32) ** level_of(streams_of[7], (MIXER_HEADS,), ((0, 4),), -0.2, 0.2), 0.5, 1.5)
    norm_gain = jnp.clip(1.0 + 0.15 * jax.random.normal(streams_of[8], (MIXER_HEADS * MHDIM,), jnp.float32), 0.25, 1.75).astype(jnp.bfloat16)
    queries = draw_queries(jax.random.fold_in(jax.random.fold_in(streams_of[11], part), 71), part)
    keys_values = draw_keys_values(jax.random.fold_in(jax.random.fold_in(streams_of[11], part), 71), part)
    return {"token_ids": token_ids, "token_tables": token_tables, "ssm_input": ssm_input, "ssm_gate": ssm_gate, "ssm_bc": ssm_bc, "conv_input": conv_input, "conv_bc": conv_bc, "skip_gain": skip_gain, "norm_gain": norm_gain, "queries": queries, "keys_values": keys_values}


EPSILON = 1e-05
HIGHEST = lax.Precision.HIGHEST

def causal_conv(values, weight):
    tap_count = weight.shape[0]
    length = values.shape[0]
    padded = jnp.concatenate([jnp.zeros((tap_count - 1,) + values.shape[1:], values.dtype), values], 0)
    summed = jnp.zeros(values.shape, jnp.float32)
    for offset in range(tap_count):
        summed = summed + weight[offset].astype(jnp.float32) * padded[offset:offset + length].astype(jnp.float32)
    return jax.nn.silu(summed).astype(jnp.bfloat16)

def block_step(state, block):
    x_block, b_block, c_block, log_block, step_block = block
    cumulative = jnp.cumsum(log_block, axis=0)
    places = jnp.arange(SPAN, dtype=jnp.int32)
    causal = (places[:, None] >= places[None, :])[:, :, None, None]
    gram_matrix = jnp.einsum('tgn,sgn->tsg', c_block.astype(jnp.float32), b_block.astype(jnp.float32))
    decays = jnp.exp(jnp.where(causal, cumulative[:, None] - cumulative[None, :], -jnp.inf))
    weights = gram_matrix[:, :, :, None] * decays * step_block[None]
    weights = lax.optimization_barrier(weights.astype(jnp.bfloat16)).astype(jnp.float32)
    inside = jnp.einsum('tsgr,sgrp->tgrp', weights, x_block.astype(jnp.float32))
    carried = jnp.exp(cumulative)[..., None] * jnp.einsum('tgn,grpn->tgrp', c_block.astype(jnp.float32), state, precision=HIGHEST)
    last_log = cumulative[-1]
    tail_weight = jnp.exp(last_log[None] - cumulative) * step_block
    new_state = jnp.exp(last_log)[..., None, None] * state + jnp.einsum('sgrp,sgn->grpn', x_block.astype(jnp.float32) * tail_weight[..., None], b_block.astype(jnp.float32), precision=HIGHEST)
    return (new_state, inside + carried)

def mamba_mixer(token_ids, token_tables, ssm_input, ssm_gate, ssm_bc, conv_input, conv_bc, skip_gain, norm_gain):
    length = ssm_input.shape[0]
    per_group = MIXER_HEADS // GROUPS
    block_count = length // SPAN
    x_conv = causal_conv(ssm_input, conv_input)
    bc_conv = causal_conv(ssm_bc, conv_bc)
    rate_values = jnp.take(token_tables[0], token_ids, axis=1).astype(jnp.float32).T
    steps = jax.nn.softplus(jnp.take(token_tables[1], token_ids, axis=1).astype(jnp.float32)).T
    x_blocks = x_conv.reshape(block_count, SPAN, GROUPS, per_group, MHDIM)
    b_blocks = bc_conv[:, 0].reshape(block_count, SPAN, GROUPS, STATE)
    c_blocks = bc_conv[:, 1].reshape(block_count, SPAN, GROUPS, STATE)
    log_blocks = (-rate_values).reshape(block_count, SPAN, GROUPS, per_group)
    step_blocks = steps.reshape(block_count, SPAN, GROUPS, per_group)
    initial = jnp.zeros((GROUPS, per_group, MHDIM, STATE), jnp.float32)
    _, outputs = lax.scan(block_step, initial, (x_blocks, b_blocks, c_blocks, log_blocks, step_blocks))
    skip_weight = skip_gain.astype(jnp.float32).reshape(GROUPS, per_group)
    mixed = outputs + skip_weight[:, :, None] * x_blocks.astype(jnp.float32)
    gate_act = jax.nn.silu(ssm_gate.astype(jnp.float32)).reshape(length, GROUPS, per_group * MHDIM)
    gated = mixed.reshape(length, GROUPS, per_group * MHDIM) * gate_act
    inverse_rms = lax.rsqrt(lax.optimization_barrier(jnp.mean(gated * gated, axis=2, keepdims=True)) + EPSILON)
    normed = (gated * inverse_rms).reshape(length, MIXER_HEADS * MHDIM) * norm_gain.astype(jnp.float32)
    return normed.astype(jnp.bfloat16)

def attention(queries, keys_values):
    length = queries.shape[0]
    query_heads = queries.reshape(length, QHEADS, HDIM)
    key_heads = keys_values[:, 0].reshape(length, KVHEADS, HDIM)
    value_heads = keys_values[:, 1].reshape(length, KVHEADS, HDIM)
    places = jnp.arange(length, dtype=jnp.int32)
    causal = places[:, None] >= places[None, :]
    factor = HDIM ** (-0.5)

    def one_head(head_index):
        group_index = head_index // (QHEADS // KVHEADS)
        query_one = lax.dynamic_index_in_dim(query_heads, head_index, 1, keepdims=False).astype(jnp.float32)
        key_one = lax.dynamic_index_in_dim(key_heads, group_index, 1, keepdims=False).astype(jnp.float32)
        value_one = lax.dynamic_index_in_dim(value_heads, group_index, 1, keepdims=False).astype(jnp.float32)
        scores = jnp.dot(query_one, key_one.T) * factor
        scores = jnp.where(causal, scores, -jnp.inf)
        highest = lax.optimization_barrier(jnp.max(scores, axis=1, keepdims=True))
        expo = jnp.exp(scores - highest)
        summed = lax.optimization_barrier(jnp.sum(expo, axis=1, keepdims=True))
        probs = lax.optimization_barrier(expo.astype(jnp.bfloat16)).astype(jnp.float32)
        return (jnp.dot(probs, value_one) / summed).astype(jnp.bfloat16)
    outputs = lax.map(one_head, jnp.arange(QHEADS, dtype=jnp.int32))
    return outputs.transpose(1, 0, 2).reshape(length, QHEADS * HDIM)

def reference(token_ids, token_tables, ssm_input, ssm_gate, ssm_bc, conv_input, conv_bc, skip_gain, norm_gain, queries, keys_values):
    mamba_out = mamba_mixer(token_ids, token_tables, ssm_input, ssm_gate, ssm_bc, conv_input, conv_bc, skip_gain, norm_gain)
    attn_out = attention(queries, keys_values)
    return (mamba_out, attn_out)
```

```python
import math

import jax
import jax.numpy as jnp
from jax import lax
from jax.experimental import pallas as pl
from jax.experimental.pallas import tpu as pltpu
from jax.sharding import PartitionSpec as P

MHDIM = 64
STATE = 256
CONV = 4
HDIM = 128
EPSILON = 1e-05
LOG2E = math.log2(math.e)
F32 = jnp.float32
BF16 = jnp.bfloat16

NY, NX, NCORE = 4, 4, 2
CHIPS = NY * NX
ROWS = 256
GROUP_CHANNELS = 2048
PAIRS = 16
EXTRA = 16
SROWS = STATE + EXTRA
MIB = 1 << 20


def params(**kw):
    return pltpu.CompilerParams(vmem_limit_bytes=56 * MIB, **kw)


def cost(flops, nbytes, trans=0):
    return pl.CostEstimate(flops=int(flops), bytes_accessed=int(nbytes), transcendentals=int(trans))


def silu(v):
    half = 0.5 * v
    return half + half * jnp.tanh(half)


def split_hi_lo(v):
    hi = v.astype(BF16)
    lo = (v - hi.astype(F32)).astype(BF16)
    return hi, lo


def table_kernel(core_ref, ids_ref, tab_ref, row_s, col_s, row_k, col_k, acc):
    step = pl.program_id(0)
    width = tab_ref.shape[2]

    @pl.when(step == 0)
    def _():
        acc[...] = jnp.zeros_like(acc)

    places = lax.broadcasted_iota(jnp.int32, (width, ROWS), 0) + step * width
    hot = jnp.where(places == ids_ref[...], 1.0, 0.0).astype(BF16)
    table = tab_ref[...].reshape(128, width)
    acc[...] += jnp.dot(table, hot, preferred_element_type=F32)

    @pl.when(step == pl.num_programs(0) - 1)
    def _():
        core = core_ref[0]
        u = lax.broadcasted_iota(jnp.int32, (ROWS, ROWS), 0)
        t = lax.broadcasted_iota(jnp.int32, (ROWS, ROWS), 1)
        tri = jnp.where(u <= t, 1.0, 0.0).astype(BF16)
        for group, row_ref, col_ref in ((1 - core, row_s, col_s), (core, row_k, col_k)):
            rate = acc[pl.ds(group * 32, 32), :]
            raw = acc[pl.ds(64 + group * 32, 32), :]
            cum = jnp.dot(rate.astype(BF16), tri, preferred_element_type=F32) * (-LOG2E)
            size = jnp.maximum(raw, 0.0) + jnp.log1p(jnp.exp(-jnp.abs(raw)))
            entry = cum - jnp.log(size) * LOG2E
            both = jnp.concatenate([cum, entry, jnp.zeros((64, ROWS), F32)], 0)
            row_ref[...] = both[:64]
            col_ref[...] = both.T


def table_call(core, token_ids, token_tables):
    width = 1024
    row = jax.ShapeDtypeStruct((64, ROWS), F32)
    col = jax.ShapeDtypeStruct((ROWS, 128), F32)
    whole = lambda shape: pl.BlockSpec(shape, lambda i, c: (0,) * len(shape))
    return pl.pallas_call(
        table_kernel,
        out_shape=(row, col, row, col),
        grid_spec=pltpu.PrefetchScalarGridSpec(
            num_scalar_prefetch=1,
            grid=(token_tables.shape[2] // width,),
            in_specs=[whole((1, ROWS)), pl.BlockSpec((2, 64, width), lambda i, c: (0, 0, i))],
            out_specs=[whole((64, ROWS)), whole((ROWS, 128))] * 2,
            scratch_shapes=[pltpu.VMEM((128, ROWS), F32)],
        ),
        compiler_params=params(),
        cost_estimate=cost(6e8, 2 * MIB),
        name="tables",
    )(core, token_ids.reshape(1, ROWS), token_tables)


def conv_block(values_ref, front_ref, taps_ref, buffer):
    width = values_ref.shape[1]
    buffer[0:16, 0:width] = front_ref[...].astype(F32)
    buffer[16 : 16 + ROWS, 0:width] = values_ref[...].astype(F32)
    taps = taps_ref[...].astype(F32)
    total = taps[CONV - 1 : CONV] * buffer[16 : 16 + ROWS, 0:width]
    for k in range(CONV - 1):
        total = total + taps[k : k + 1] * buffer[13 + k : 13 + k + ROWS, 0:width]
    return silu(total).astype(BF16)


def state_kernel(
    group_ref,
    x_ref,
    xf_ref,
    xt_ref,
    b_ref,
    bf_ref,
    bt_ref,
    c_ref,
    cf_ref,
    ct_ref,
    col_ref,
    xc_ref,
    bc_ref,
    cc_ref,
    s_ref,
    buffer,
    btrans,
):
    j = pl.program_id(0)

    @pl.when(j == 0)
    def _():
        b = conv_block(b_ref, bf_ref, bt_ref, buffer)
        bc_ref[...] = b
        btrans[...] = b.astype(F32).T.astype(BF16)
        cc_ref[...] = conv_block(c_ref, cf_ref, ct_ref, buffer)

    x = conv_block(x_ref, xf_ref, xt_ref, buffer)
    xc_ref[...] = x
    last = col_ref[ROWS - 1 : ROWS, 0:32]
    tail = jnp.exp2(last - col_ref[:, 32:64])
    whole = jnp.broadcast_to(jnp.exp2(last), (EXTRA, 32))
    hi, lo = split_hi_lo(jnp.concatenate([tail, whole], 0))
    r = lax.broadcasted_iota(jnp.int32, (32, 512), 0)
    ch = lax.broadcasted_iota(jnp.int32, (32, 512), 1)
    hot = jnp.where(r == j * 8 + ch // MHDIM, 1.0, 0.0).astype(BF16)
    wide = jnp.dot(hi, hot, preferred_element_type=F32) + jnp.dot(
        lo, hot, preferred_element_type=F32
    )
    scaled = (x.astype(F32) * wide[:ROWS]).astype(BF16)
    state = jnp.dot(btrans[...], scaled, preferred_element_type=F32)
    edge_hi, edge_lo = split_hi_lo(wide[ROWS:])
    place = lax.broadcasted_iota(jnp.int32, (EXTRA, 512), 0)
    edge = jnp.where(
        place == 0,
        edge_hi.astype(F32),
        jnp.where(place == 1, edge_lo.astype(F32), 0.0),
    ).astype(BF16)
    for p in range(4):
        s_ref[p, 0:STATE, :] = state[:, p * 128 : (p + 1) * 128].astype(BF16)
        s_ref[p, STATE:SROWS, :] = edge[:, p * 128 : (p + 1) * 128]


def state_call(group, ssm_input, front, conv_input, bc, conv_bc, col):
    wide = lambda rows: pl.BlockSpec((rows, 512), lambda j, g: (0, g[0] * 4 + j))
    front_wide = pl.BlockSpec((16, 512), lambda j, g: (0, g[0] * 4 + j))
    b = lambda rows: pl.BlockSpec((rows, STATE), lambda j, g: (0, g[0]))
    c = lambda rows: pl.BlockSpec((rows, STATE), lambda j, g: (0, 2 + g[0]))
    bfront = pl.BlockSpec((16, STATE), lambda j, g: (0, 16 + g[0]))
    cfront = pl.BlockSpec((16, STATE), lambda j, g: (0, 18 + g[0]))
    fixed = lambda shape: pl.BlockSpec(shape, lambda j, g: (0,) * len(shape))
    return pl.pallas_call(
        state_kernel,
        out_shape=(
            jax.ShapeDtypeStruct((ROWS, GROUP_CHANNELS), BF16),
            jax.ShapeDtypeStruct((ROWS, STATE), BF16),
            jax.ShapeDtypeStruct((ROWS, STATE), BF16),
            jax.ShapeDtypeStruct((PAIRS, SROWS, 128), BF16),
        ),
        grid_spec=pltpu.PrefetchScalarGridSpec(
            num_scalar_prefetch=1,
            grid=(4,),
            in_specs=[
                wide(ROWS),
                front_wide,
                wide(CONV),
                b(ROWS),
                bfront,
                b(CONV),
                c(ROWS),
                cfront,
                c(CONV),
                fixed((ROWS, 128)),
            ],
            out_specs=[
                pl.BlockSpec((ROWS, 512), lambda j, g: (0, j)),
                fixed((ROWS, STATE)),
                fixed((ROWS, STATE)),
                pl.BlockSpec((4, SROWS, 128), lambda j, g: (j, 0, 0)),
            ],
            scratch_shapes=[pltpu.VMEM((16 + ROWS, 512), F32), pltpu.VMEM((STATE, ROWS), BF16)],
        ),
        compiler_params=params(),
        cost_estimate=cost(5e9, 3 * MIB),
        name="conv_state",
    )(group, ssm_input, front, conv_input, bc, front, conv_bc, bc, front, conv_bc, col)


def inside_kernel(x_ref, b_ref, c_ref, row_ref, col_ref, skip_ref, y_ref, gram):
    j = pl.program_id(0)

    @pl.when(j == 0)
    def _():
        product = lax.dot_general(
            c_ref[...], b_ref[...], (((1,), (1,)), ((), ())), preferred_element_type=F32
        )
        t = lax.broadcasted_iota(jnp.int32, (ROWS, ROWS), 0)
        s = lax.broadcasted_iota(jnp.int32, (ROWS, ROWS), 1)
        gram[...] = jnp.where(s <= t, product, 0.0)

    columns = pltpu.roll(col_ref[...], lax.rem(128 - j * 8, 128), 1)
    entries = row_ref[pl.ds(pl.multiple_of(32 + j * 8, 8), 8), :]
    lane = lax.broadcasted_iota(jnp.int32, (ROWS, 128), 1)
    for p in range(4):
        x = x_ref[:, p * 128 : (p + 1) * 128]
        parts = []
        for h in (2 * p, 2 * p + 1):
            power = jnp.minimum(columns[:, h : h + 1] - entries[h : h + 1, :], 1.0)
            weight = (gram[...] * jnp.exp2(power)).astype(BF16)
            parts.append(jnp.dot(weight, x, preferred_element_type=F32))
        y = jnp.where(lane < MHDIM, parts[0], parts[1])
        y = y + skip_ref[:, p * 128 : (p + 1) * 128] * x.astype(F32)
        y_ref[:, p * 128 : (p + 1) * 128] = y.astype(BF16)


def inside_call(group, x, b, c, row, col, skip):
    fixed = lambda shape: pl.BlockSpec(shape, lambda j, g: (0,) * len(shape))
    return pl.pallas_call(
        lambda g, *refs: inside_kernel(*refs),
        out_shape=jax.ShapeDtypeStruct((ROWS, GROUP_CHANNELS), BF16),
        grid_spec=pltpu.PrefetchScalarGridSpec(
            num_scalar_prefetch=1,
            grid=(4,),
            in_specs=[
                pl.BlockSpec((ROWS, 512), lambda j, g: (0, j)),
                fixed((ROWS, STATE)),
                fixed((ROWS, STATE)),
                fixed((64, ROWS)),
                fixed((ROWS, 128)),
                pl.BlockSpec((1, 512), lambda j, g: (0, g[0] * 4 + j)),
            ],
            out_specs=pl.BlockSpec((ROWS, 512), lambda j, g: (0, j)),
            scratch_shapes=[pltpu.VMEM((ROWS, ROWS), F32)],
        ),
        compiler_params=params(),
        cost_estimate=cost(4e9, 3 * MIB),
        name="inside",
    )(group, x, b, c, row, col, skip)


def edge_of(s):
    return s[STATE : STATE + 1, :].astype(F32) + s[STATE + 1 : STATE + 2, :].astype(F32)


def combine_kernel(core_ref, own_ref, other_ref, out_ref):
    first_is_own = core_ref[0] == 0
    place = lax.broadcasted_iota(jnp.int32, (EXTRA, 128), 0)
    for p in range(own_ref.shape[0]):
        own, other = own_ref[p].astype(F32), other_ref[p].astype(F32)
        first = jnp.where(first_is_own, own, other)
        second = jnp.where(first_is_own, other, own)
        later = edge_of(second)
        out_ref[p, 0:STATE, :] = (later * first[:STATE] + second[:STATE]).astype(BF16)
        hi, lo = split_hi_lo(later * edge_of(first))
        out_ref[p, STATE:SROWS, :] = jnp.where(
            place == 0, hi.astype(F32), jnp.where(place == 1, lo.astype(F32), 0.0)
        ).astype(BF16)


def combine_call(core, own, other):
    spec = pl.BlockSpec((4, SROWS, 128), lambda j, c: (j, 0, 0))
    return pl.pallas_call(
        combine_kernel,
        out_shape=jax.ShapeDtypeStruct((PAIRS, SROWS, 128), BF16),
        grid_spec=pltpu.PrefetchScalarGridSpec(
            num_scalar_prefetch=1, grid=(4,), in_specs=[spec, spec], out_specs=spec
        ),
        compiler_params=params(),
        cost_estimate=cost(1e9, 3 * MIB),
        name="combine",
    )(core, own, other)


def prefix_kernel(s_ref, out_ref):
    carried = jnp.zeros((STATE, 128), F32)
    for k in range(CHIPS):
        out_ref[k] = carried.astype(BF16)
        if k < CHIPS - 1:
            s = s_ref[k].astype(F32)
            carried = edge_of(s) * carried + s[:STATE]


def prefix_call(s):
    return pl.pallas_call(
        prefix_kernel,
        out_shape=jax.ShapeDtypeStruct((CHIPS, STATE, 128), BF16),
        in_specs=[pl.BlockSpec(memory_space=pltpu.VMEM)],
        out_specs=pl.BlockSpec(memory_space=pltpu.VMEM),
        compiler_params=params(),
        cost_estimate=cost(1e9, 2 * MIB),
        name="prefix",
    )(s)


def enter_kernel(core_ref, own_ref, other_ref, in_ref, keep_ref, send_ref):
    core = core_ref[0]
    for p in range(own_ref.shape[0]):
        first = jnp.where(core == 0, own_ref[p].astype(F32), other_ref[p].astype(F32))
        entering = in_ref[p].astype(F32)
        later = edge_of(first) * entering + first[:STATE]
        keep_ref[p] = jnp.where(core == 0, entering, later).astype(BF16)
        send_ref[p] = jnp.where(core == 0, later, entering).astype(BF16)


def enter_call(core, own, other, entering):
    spec = pl.BlockSpec((4, SROWS, 128), lambda j, c: (j, 0, 0))
    short = pl.BlockSpec((4, STATE, 128), lambda j, c: (j, 0, 0))
    shape = jax.ShapeDtypeStruct((PAIRS, STATE, 128), BF16)
    return pl.pallas_call(
        enter_kernel,
        out_shape=(shape, shape),
        grid_spec=pltpu.PrefetchScalarGridSpec(
            num_scalar_prefetch=1,
            grid=(4,),
            in_specs=[spec, spec, short],
            out_specs=[short, short],
        ),
        compiler_params=params(),
        cost_estimate=cost(1e9, 4 * MIB),
        name="enter",
    )(core, own, other, entering)


def output_kernel(g_ref, s_ref, c_ref, col_ref, y_ref, gate_ref, gain_ref, old_ref, out_ref, held):
    rows = c_ref.shape[0]
    c = c_ref[...]
    grown = jnp.exp2(col_ref[:, 0:32])
    lane = lax.broadcasted_iota(jnp.int32, (rows, 128), 1)
    squares = jnp.zeros((rows, 128), F32)
    for p in range(PAIRS):
        at = slice(p * 128, (p + 1) * 128)
        carried = jnp.dot(c, s_ref[p], preferred_element_type=F32)
        factor = jnp.where(
            lane < MHDIM, grown[:, 2 * p : 2 * p + 1], grown[:, 2 * p + 1 : 2 * p + 2]
        )
        y = y_ref[:, at].astype(F32) + factor * carried
        gated = y * silu(gate_ref[:, at].astype(F32))
        squares = squares + gated * gated
        held[:, at] = gated
    mean = jnp.sum(squares, axis=1, keepdims=True) * (1.0 / GROUP_CHANNELS)
    scale = lax.rsqrt(mean + EPSILON)
    for p in range(PAIRS):
        at = slice(p * 128, (p + 1) * 128)
        out_ref[:, at] = (held[:, at] * scale * gain_ref[:, at].astype(F32)).astype(BF16)


def output_call(group, state, c, col, y, gate, gain, old):
    rows = 128
    in_specs = [
        pl.BlockSpec((PAIRS, STATE, 128), lambda i, g: (0, 0, 0)),
        pl.BlockSpec((rows, STATE), lambda i, g: (i, 0)),
        pl.BlockSpec((rows, 128), lambda i, g: (i, 0)),
        pl.BlockSpec((rows, GROUP_CHANNELS), lambda i, g: (i, 0)),
        pl.BlockSpec((rows, GROUP_CHANNELS), lambda i, g: (i, g[0])),
        pl.BlockSpec((1, GROUP_CHANNELS), lambda i, g: (0, g[0])),
    ]
    args = [group, state, c, col, y, gate, gain]
    if old is None:
        body = lambda *r: output_kernel(*r[:7], None, *r[7:])
        aliases = {}
    else:
        body = output_kernel
        in_specs.append(pl.BlockSpec(memory_space=pl.ANY))
        args.append(old)
        aliases = {7: 0}
    return pl.pallas_call(
        body,
        out_shape=jax.ShapeDtypeStruct((ROWS, 2 * GROUP_CHANNELS), BF16),
        grid_spec=pltpu.PrefetchScalarGridSpec(
            num_scalar_prefetch=1,
            grid=(ROWS // rows,),
            in_specs=in_specs,
            out_specs=pl.BlockSpec((rows, GROUP_CHANNELS), lambda i, g: (i, g[0])),
            scratch_shapes=[pltpu.VMEM((rows, GROUP_CHANNELS), F32)],
        ),
        input_output_aliases=aliases,
        compiler_params=params(),
        cost_estimate=cost(3e9, 5 * MIB),
        name="mixer_out",
    )(*args)


UNIT = 512
QPER = 8
SCALE = LOG2E * HDIM ** (-0.5)


def attention_kernel(sizes, start, has_acc, final, has_old, *refs):
    scal, q_ref = refs[:2]
    refs = list(refs[2:])
    pieces = [refs.pop(0) for _ in sizes]
    acc_in = refs.pop(0) if has_acc else None
    if has_old:
        refs.pop(0)
    out_ref, kv, qs = refs[:3]
    acc = refs[3] if final else out_ref
    sem = refs[-1]
    chip, core = scal[1], scal[2]
    count = sum(sizes)
    copies = []
    offset = 0
    for i, (piece, n) in enumerate(zip(pieces, sizes)):
        copies.append(pltpu.make_async_copy(piece, kv.at[pl.ds(offset, n)], sem.at[i]))
        offset += n
    for copy in copies:
        copy.start()
    for h in range(QPER):
        hi, lo = split_hi_lo(q_ref[:, h * HDIM : (h + 1) * HDIM].astype(F32) * SCALE)
        qs[h, :, 0:HDIM] = hi
        qs[h, :, HDIM:] = lo
    if has_acc:
        acc[...] = acc_in[...]
    else:
        acc[...] = jnp.zeros_like(acc)
    for copy in copies:
        copy.wait()

    def scores_of(h, keys):
        return lax.dot_general(
            qs[h], keys, (((1,), (1,)), ((), ())), preferred_element_type=F32
        )

    def keys_values_of(u):
        block = kv[u]
        keys = jnp.concatenate([block[:, :HDIM], block[:, :HDIM]], 1)
        values = jnp.concatenate([block[:, HDIM:], jnp.ones((UNIT, HDIM), BF16)], 1)
        return keys, values

    def visible_in(shift):
        row = lax.broadcasted_iota(jnp.int32, (ROWS, UNIT), 0) + core * ROWS
        col = lax.broadcasted_iota(jnp.int32, (ROWS, UNIT), 1)
        return col + shift <= row

    def absorb(u, masked):
        keys, values = keys_values_of(u)
        for h in range(QPER):
            p = jnp.exp2(scores_of(h, keys))
            if masked:
                p = jnp.where(visible_in(0), p, 0.0)
            acc[h] += jnp.dot(p.astype(BF16), values, preferred_element_type=F32)

    def one(u, carry):
        unit = scal[3 + u]

        @pl.when(unit < chip)
        def _():
            absorb(u, False)

        @pl.when(unit == chip)
        def _():
            absorb(u, True)

        return carry

    lax.fori_loop(start, count, one, 0)
    if not final:
        return

    least = jnp.full((ROWS, HDIM), 1.0, F32)
    most = jnp.full((ROWS, HDIM), 1.0, F32)
    for h in range(QPER):
        total = acc[h, :, HDIM:]
        least = jnp.minimum(least, total)
        most = jnp.maximum(most, total)
        out_ref[:, h * HDIM : (h + 1) * HDIM] = (acc[h, :, :HDIM] / total).astype(BF16)
    safe = (jnp.min(least) > 2.0**-80) & (jnp.max(most) < 2.0**110)

    @pl.when(jnp.logical_not(safe))
    def _():
        def head(h, carry):
            def unit_step(u, state):
                top, total, summed = state
                keys, values = keys_values_of(u)
                shown = visible_in((scal[3 + u] - chip) * UNIT)
                scores = jnp.where(shown, scores_of(h, keys), -1e30)
                new_top = jnp.maximum(top, jnp.max(scores, axis=1, keepdims=True))
                shrink = jnp.exp2(top - new_top)
                p = jnp.where(shown, jnp.exp2(scores - new_top), 0.0)
                total = total * shrink + jnp.sum(p, axis=1, keepdims=True)
                summed = summed * shrink + jnp.dot(
                    p.astype(BF16), values[:, :HDIM], preferred_element_type=F32
                )
                return new_top, total, summed

            zero = jnp.zeros((ROWS, 1), F32)
            state = (zero - 1e30, zero, jnp.zeros((ROWS, HDIM), F32))
            _, total, summed = lax.fori_loop(0, count, unit_step, state)
            out_ref[:, pl.ds(pl.multiple_of(h * HDIM, HDIM), HDIM)] = (summed / total).astype(BF16)
            return carry

        lax.fori_loop(0, QPER, head, 0)


def attention_call(scal, queries, pieces, start, acc, final, old):
    sizes = [p.shape[0] for p in pieces]
    count = sum(sizes)
    width = QPER * HDIM
    whole = pl.BlockSpec((QPER, ROWS, 2 * HDIM), lambda i, s: (0, 0, 0))
    anywhere = pl.BlockSpec(memory_space=pl.ANY)
    in_specs = [pl.BlockSpec((ROWS, width), lambda i, s: (0, s[0]))] + [anywhere] * len(sizes)
    args = [scal, queries, *pieces]
    if acc is not None:
        in_specs.append(whole)
        args.append(acc)
    aliases = {}
    if old is not None:
        in_specs.append(anywhere)
        aliases = {len(args): 0}
        args.append(old)
    acc_shape = (QPER, ROWS, 2 * HDIM)
    if final:
        out_shape = jax.ShapeDtypeStruct((ROWS, 2 * width), BF16)
        out_specs = pl.BlockSpec((ROWS, width), lambda i, s: (0, s[0]))
    else:
        out_shape = jax.ShapeDtypeStruct(acc_shape, F32)
        out_specs = whole
    scratch = [pltpu.VMEM((count, UNIT, 2 * HDIM), BF16), pltpu.VMEM((QPER, ROWS, 2 * HDIM), BF16)]
    if final:
        scratch.append(pltpu.VMEM(acc_shape, F32))
    scratch.append(pltpu.SemaphoreType.DMA((len(sizes),)))

    def body(*refs):
        attention_kernel(sizes, start, acc is not None, final, old is not None, *refs)

    return pl.pallas_call(
        body,
        out_shape=out_shape,
        grid_spec=pltpu.PrefetchScalarGridSpec(
            num_scalar_prefetch=1,
            grid=(1,),
            in_specs=in_specs,
            out_specs=out_specs,
            scratch_shapes=scratch,
        ),
        input_output_aliases=aliases,
        compiler_params=params(),
        cost_estimate=cost(1.2e9 * (count - start), 4 * MIB),
        name="attention",
    )(*args)


def permute(value, target):
    pairs = []
    for place in range(NY * NX * NCORE):
        y, x, c = place // (NX * NCORE), (place // NCORE) % NX, place % NCORE
        y, x, c = target(y, x, c)
        pairs.append((place, ((y % NY) * NX + x % NX) * NCORE + c))
    return lax.ppermute(value, "seq", pairs)


def swap(value):
    return permute(value, lambda y, x, c: (y, x, 1 - c))


def along(value, step, second):
    def target(y, x, c):
        return (y, x + step, c) if c == second else (y + step, x, c)

    return permute(value, target)


def ring_gather(value, second):
    half = value.shape[0] // 2
    left = along(value, 1, second)
    right = along(value, -1, second)
    far_first = along(left[:half], 1, second)
    far_last = along(right[half:], -1, second)
    return left, right, far_first, far_last


def unit_ids(y, x, x_first):
    ids = []
    for two in (0, -1, 1, 2):
        for one in (0, -1, 1, 2):
            across = ((y + two) % NY) * NX + (x + one) % NX
            down = ((y + one) % NY) * NX + (x + two) % NX
            ids.append(jnp.where(x_first, across, down))
    return ids


ALL_CHIPS = [[chip * NCORE + core for chip in range(CHIPS)] for core in range(NCORE)]


def exchange(value):
    return lax.all_to_all(value, "seq", 0, 0, axis_index_groups=ALL_CHIPS, tiled=True)


def local(
    token_ids,
    token_tables,
    ssm_input,
    ssm_gate,
    ssm_bc,
    conv_input,
    conv_bc,
    skip_gain,
    norm_gain,
    queries,
    keys_values,
):
    place = lax.axis_index("seq")
    core = lax.rem(place, NCORE)
    chip = place // NCORE
    y, x = chip // NX, lax.rem(chip, NX)
    keep, send = core.reshape(1), (1 - core).reshape(1)

    bc = ssm_bc.reshape(ROWS, -1)
    edge = jnp.concatenate([ssm_input[ROWS - 16 :], bc[ROWS - 16 :]], 1)
    seq = NY * NX * NCORE
    front = lax.ppermute(edge, "seq", [(i, i + 1) for i in range(seq - 1)])

    kv = keys_values.reshape(ROWS, 4, HDIM)
    zero = jnp.concatenate([kv[:, 0], kv[:, 2]], 1)
    one = jnp.concatenate([kv[:, 1], kv[:, 3]], 1)
    mine = jnp.where(core == 0, zero, one)
    from_other = swap(jnp.where(core == 0, one, zero))
    unit = jnp.where(
        core == 0,
        jnp.concatenate([mine, from_other], 0),
        jnp.concatenate([from_other, mine], 0),
    )
    left, right, far_first, far_last = ring_gather(unit, 0)
    line = jnp.concatenate([unit, left, right, far_first, far_last], 0).reshape(4, UNIT, 2 * HDIM)
    pieces = [line, *ring_gather(line, 1)]
    others = [swap(p) for p in pieces]
    ids_mine = unit_ids(y, x, core == 0)
    ids_other = unit_ids(y, x, core == 1)
    scal_mine = jnp.stack([core, chip, core, *ids_mine]).astype(jnp.int32)
    scal_other = jnp.stack([1 - core, chip, core, *ids_other]).astype(jnp.int32)

    row_s, col_s, row_k, col_k = table_call(keep, token_ids, token_tables)
    taps_bc = conv_bc.reshape(CONV, -1)
    x_s, b_s, c_s, state_s = state_call(send, ssm_input, front, conv_input, bc, taps_bc, col_s)
    state_o = swap(state_s)
    x_k, b_k, c_k, state_k = state_call(keep, ssm_input, front, conv_input, bc, taps_bc, col_k)
    joined = combine_call(keep, state_k, state_o)
    entering = exchange(prefix_call(exchange(joined)))
    state_in_k, state_to_other = enter_call(keep, state_k, state_o, entering)
    state_in_s = swap(state_to_other)

    skip = jnp.repeat(skip_gain, MHDIM).reshape(1, -1)
    y_s = inside_call(send, x_s, b_s, c_s, row_s, col_s, skip)
    y_k = inside_call(keep, x_k, b_k, c_k, row_k, col_k, skip)
    acc = attention_call(scal_mine, queries, pieces[:1], 0, None, False, None)
    attn = attention_call(scal_mine, queries, pieces, 4, acc, True, None)
    attn = attention_call(scal_other, queries, others, 0, None, True, attn)

    gain = norm_gain.reshape(1, -1)
    mixed = output_call(keep, state_in_k, c_k, col_k, y_k, ssm_gate, gain, None)
    mixed = output_call(send, state_in_s, c_s, col_s, y_s, ssm_gate, gain, mixed)
    return mixed, attn


def solution(mesh):
    in_specs = (
        P(("dp", "seq")),
        P(None, "head", None),
        P(("dp", "seq"), "head"),
        P(("dp", "seq"), "head"),
        P(("dp", "seq"), None, "head"),
        P(None, "head"),
        P(None, None, "head"),
        P("head"),
        P("head"),
        P(("dp", "seq"), "head"),
        P(("dp", "seq"), None, "head"),
    )
    out_specs = (P(("dp", "seq"), "head"), P(("dp", "seq"), "head"))
    return jax.shard_map(local, mesh=mesh, in_specs=in_specs, out_specs=out_specs, check_vma=False)
```

```python
import math

import jax
import jax.numpy as jnp
from jax import lax
from jax.experimental import pallas as pl
from jax.experimental.pallas import tpu as pltpu
from jax.sharding import PartitionSpec as P

MHDIM = 64
STATE = 256
CONV = 4
HDIM = 128
EPSILON = 1e-05
LOG2E = math.log2(math.e)
F32 = jnp.float32
BF16 = jnp.bfloat16

NY, NX, NCORE = 4, 4, 2
CHIPS = NY * NX
ROWS = 256
GROUP_CHANNELS = 2048
PAIRS = 16
EXTRA = 16
SROWS = STATE + EXTRA
MIB = 1 << 20


def params(mib=16):
    return pltpu.CompilerParams(vmem_limit_bytes=mib * MIB)


def cost(flops, nbytes, trans=0):
    return pl.CostEstimate(flops=int(flops), bytes_accessed=int(nbytes), transcendentals=int(trans))


def silu(v):
    half = 0.5 * v
    return half + half * jnp.tanh(half)


def split_hi_lo(v):
    hi = v.astype(BF16)
    lo = (v - hi.astype(F32)).astype(BF16)
    return hi, lo


def table_kernel(ids_ref, tab_ref, row_ref, col_ref, acc):
    step = pl.program_id(0)
    width = tab_ref.shape[2]

    @pl.when(step == 0)
    def _():
        acc[...] = jnp.zeros_like(acc)

    part = 1024
    for i in range(width // part):
        places = lax.broadcasted_iota(jnp.int32, (part, ROWS), 0) + (step * width + i * part)
        hot = jnp.where(places == ids_ref[...], 1.0, 0.0).astype(BF16)
        table = tab_ref[:, :, i * part : (i + 1) * part].reshape(128, part)
        acc[...] += jnp.dot(table, hot, preferred_element_type=F32)

    @pl.when(step == pl.num_programs(0) - 1)
    def _():
        u = lax.broadcasted_iota(jnp.int32, (ROWS, ROWS), 0)
        t = lax.broadcasted_iota(jnp.int32, (ROWS, ROWS), 1)
        tri = jnp.where(u <= t, 1.0, 0.0).astype(BF16)
        rate, raw = acc[0:64, :], acc[64:128, :]
        cum = jnp.dot(rate.astype(BF16), tri, preferred_element_type=F32) * (-LOG2E)
        size = jnp.maximum(raw, 0.0) + jnp.log1p(jnp.exp(-jnp.abs(raw)))
        both = jnp.concatenate([cum, cum - jnp.log(size) * LOG2E], 0)
        row_ref[...] = both
        col_ref[...] = both.T


def table_call(token_ids, token_tables):
    width = 4096
    return pl.pallas_call(
        table_kernel,
        out_shape=(
            jax.ShapeDtypeStruct((128, ROWS), F32),
            jax.ShapeDtypeStruct((ROWS, 128), F32),
        ),
        grid=(token_tables.shape[2] // width,),
        in_specs=[
            pl.BlockSpec((1, ROWS), lambda i: (0, 0)),
            pl.BlockSpec((2, 64, width), lambda i: (0, 0, i)),
        ],
        out_specs=[
            pl.BlockSpec((128, ROWS), lambda i: (0, 0)),
            pl.BlockSpec((ROWS, 128), lambda i: (0, 0)),
        ],
        scratch_shapes=[pltpu.VMEM((128, ROWS), F32)],
        compiler_params=params(),
        cost_estimate=cost(4e9, 2 * MIB),
        name="tables",
    )(token_ids.reshape(1, ROWS), token_tables)


def spread(values, first_head, width):
    hi, lo = split_hi_lo(values)
    r = lax.broadcasted_iota(jnp.int32, (64, width), 0)
    ch = lax.broadcasted_iota(jnp.int32, (64, width), 1)
    hot = jnp.where(r == first_head + ch // MHDIM, 1.0, 0.0).astype(BF16)
    return jnp.dot(
        jnp.concatenate([hi, lo], 1),
        jnp.concatenate([hot, hot], 0),
        preferred_element_type=F32,
    )


LANES = 128
STRIP = 64


def conv_strips(values_ref, front_ref, taps_ref, at, buffer, out_ref):
    buffer[0:16, :] = front_ref[:, at].astype(F32)
    for r in range(0, ROWS, STRIP):
        buffer[16 + r : 16 + r + STRIP, :] = values_ref[r : r + STRIP, at].astype(F32)
    taps = taps_ref[:, at].astype(F32)
    for r in range(0, ROWS, STRIP):
        total = taps[CONV - 1 : CONV] * buffer[16 + r : 16 + r + STRIP, :]
        for k in range(CONV - 1):
            total = total + taps[k : k + 1] * buffer[13 + k + r : 13 + k + r + STRIP, :]
        out_ref[r : r + STRIP, at] = silu(total).astype(BF16)


def state_kernel(group_ref, *refs):
    x_ref, xf_ref, xt_ref, b_ref, bf_ref, bt_ref, c_ref, cf_ref, ct_ref, col_ref = refs[:10]
    xc_ref, bc_ref, cc_ref, s_ref, buffer, scaled = refs[10:]
    group = group_ref[0]
    for i in range(STATE // LANES):
        at = slice(i * LANES, (i + 1) * LANES)
        conv_strips(b_ref, bf_ref, bt_ref, at, buffer.at[i], bc_ref)
        conv_strips(c_ref, cf_ref, ct_ref, at, buffer.at[2 + i], cc_ref)
    btrans = bc_ref[...].astype(F32).T.astype(BF16)
    last = col_ref[ROWS - 1 : ROWS, 0:64]
    tail = jnp.exp2(last - col_ref[:, 64:128])
    weights = jnp.concatenate([tail, jnp.broadcast_to(jnp.exp2(last), (EXTRA, 64))], 0)
    place = lax.broadcasted_iota(jnp.int32, (EXTRA, LANES), 0)
    for p in range(PAIRS):
        at = slice(p * LANES, (p + 1) * LANES)
        conv_strips(x_ref, xf_ref, xt_ref, at, buffer.at[p % 4], xc_ref)
        wide = spread(weights, group * 32 + 2 * p, LANES)
        for r in range(0, ROWS, STRIP):
            rows = slice(r, r + STRIP)
            scaled[p % 4, rows, :] = (xc_ref[rows, at].astype(F32) * wide[rows]).astype(BF16)
        state = jnp.dot(btrans, scaled[p % 4], preferred_element_type=F32)
        s_ref[p, 0:STATE, :] = state.astype(BF16)
        hi, lo = split_hi_lo(wide[ROWS:])
        edge = jnp.where(place == 0, hi.astype(F32), jnp.where(place == 1, lo.astype(F32), 0.0))
        s_ref[p, STATE:SROWS, :] = edge.astype(BF16)


def state_call(group, ssm_input, front, conv_input, bc, conv_bc, col):
    wide = lambda rows: pl.BlockSpec((rows, GROUP_CHANNELS), lambda j, g: (0, g[0]))
    narrow = lambda rows, base: pl.BlockSpec((rows, STATE), lambda j, g: (0, base + g[0]))
    whole = lambda shape: pl.BlockSpec(shape, lambda j, g: (0,) * len(shape))
    shapes = ((ROWS, GROUP_CHANNELS), (ROWS, STATE), (ROWS, STATE), (PAIRS, SROWS, 128))
    return pl.pallas_call(
        state_kernel,
        out_shape=tuple(jax.ShapeDtypeStruct(shape, BF16) for shape in shapes),
        grid_spec=pltpu.PrefetchScalarGridSpec(
            num_scalar_prefetch=1,
            grid=(1,),
            in_specs=[
                wide(ROWS),
                wide(16),
                wide(CONV),
                narrow(ROWS, 0),
                narrow(16, 16),
                narrow(CONV, 0),
                narrow(ROWS, 2),
                narrow(16, 18),
                narrow(CONV, 2),
                whole((ROWS, 128)),
            ],
            out_specs=[whole(shape) for shape in shapes],
            scratch_shapes=[
                pltpu.VMEM((4, 16 + ROWS, LANES), F32),
                pltpu.VMEM((4, ROWS, LANES), BF16),
            ],
        ),
        compiler_params=params(),
        cost_estimate=cost(4e9, 3 * MIB),
        name="conv_state",
    )(group, ssm_input, front, conv_input, bc, front, conv_bc, bc, front, conv_bc, col)


def inside_kernel(g_ref, x_ref, b_ref, c_ref, row_ref, col_ref, skip_ref, y_ref, gram, held):
    g = g_ref[0]
    half = ROWS // 2
    product = lax.dot_general(
        c_ref[...], b_ref[...], (((1,), (1,)), ((), ())), preferred_element_type=F32
    )
    t = lax.broadcasted_iota(jnp.int32, (ROWS, ROWS), 0)
    s = lax.broadcasted_iota(jnp.int32, (ROWS, ROWS), 1)
    gram[...] = jnp.where(s <= t, product, 0.0)
    columns = pltpu.roll(col_ref[...], lax.rem(128 - g * 32, 128), 1)
    lane = lax.broadcasted_iota(jnp.int32, (half, LANES), 1)
    for p in range(PAIRS):
        at = slice(p * LANES, (p + 1) * LANES)
        for i in range(2):
            h = 2 * p + i
            entries = row_ref[pl.ds(64 + g * 32 + h, 1), :]
            slot = held.at[2 * (p % 2) + i]
            for r in range(0, ROWS, STRIP):
                width = half if r < half else ROWS
                power = columns[r : r + STRIP, h : h + 1] - entries[:, :width]
                weight = gram[r : r + STRIP, :width] * jnp.exp2(jnp.minimum(power, 1.0))
                slot[r : r + STRIP, :width] = weight.astype(BF16)
        head = g * 32 + 2 * p
        skip = jnp.where(lane[0:1] < MHDIM, skip_ref[head], skip_ref[head + 1])
        for r, width in ((0, half), (half, ROWS)):
            first, second = (
                jnp.dot(
                    held[2 * (p % 2) + i, r : r + half, :width],
                    x_ref[:width, at],
                    preferred_element_type=F32,
                )
                for i in range(2)
            )
            rows = slice(r, r + half)
            y = jnp.where(lane < MHDIM, first, second) + skip * x_ref[rows, at].astype(F32)
            y_ref[rows, at] = y.astype(BF16)


def inside_call(group, x, b, c, row, col, skip):
    vmem = pl.BlockSpec(memory_space=pltpu.VMEM)
    smem = pl.BlockSpec(memory_space=pltpu.SMEM)
    return pl.pallas_call(
        inside_kernel,
        out_shape=jax.ShapeDtypeStruct((ROWS, GROUP_CHANNELS), BF16),
        in_specs=[smem, vmem, vmem, vmem, vmem, vmem, smem],
        out_specs=vmem,
        scratch_shapes=[pltpu.VMEM((ROWS, ROWS), F32), pltpu.VMEM((4, ROWS, ROWS), BF16)],
        compiler_params=params(),
        cost_estimate=cost(5e9, 3 * MIB),
        name="inside",
    )(group, x, b, c, row, col, skip)


def edge_of(s):
    return s[STATE : STATE + 1, :].astype(F32) + s[STATE + 1 : STATE + 2, :].astype(F32)


def combine_kernel(core_ref, own_ref, other_ref, out_ref):
    own_first = core_ref[0] == 0
    place = lax.broadcasted_iota(jnp.int32, (EXTRA, 128), 0)
    for p in range(PAIRS):
        own_edge, other_edge = edge_of(own_ref[p]), edge_of(other_ref[p])
        keep_own = jnp.where(own_first, other_edge, 1.0)
        keep_other = jnp.where(own_first, 1.0, own_edge)
        for r in range(0, STATE, STRIP):
            rows = slice(r, r + STRIP)
            own, other = own_ref[p, rows].astype(F32), other_ref[p, rows].astype(F32)
            out_ref[p, rows, :] = (keep_own * own + keep_other * other).astype(BF16)
        hi, lo = split_hi_lo(own_edge * other_edge)
        out_ref[p, STATE:SROWS, :] = jnp.where(
            place == 0, hi.astype(F32), jnp.where(place == 1, lo.astype(F32), 0.0)
        ).astype(BF16)


def combine_call(core, own, other):
    vmem = pl.BlockSpec(memory_space=pltpu.VMEM)
    return pl.pallas_call(
        combine_kernel,
        out_shape=jax.ShapeDtypeStruct((PAIRS, SROWS, 128), BF16),
        in_specs=[pl.BlockSpec(memory_space=pltpu.SMEM), vmem, vmem],
        out_specs=vmem,
        compiler_params=params(),
        cost_estimate=cost(2e9, 3 * MIB),
        name="combine",
    )(core, own, other)


def prefix_kernel(s_ref, out_ref):
    carried = jnp.zeros((STATE, 128), F32)
    for k in range(CHIPS):
        out_ref[k] = carried.astype(BF16)
        if k < CHIPS - 1:
            s = s_ref[k].astype(F32)
            carried = edge_of(s_ref[k]) * carried + s[:STATE]


def prefix_call(s):
    return pl.pallas_call(
        prefix_kernel,
        out_shape=jax.ShapeDtypeStruct((CHIPS, STATE, 128), BF16),
        in_specs=[pl.BlockSpec(memory_space=pltpu.VMEM)],
        out_specs=pl.BlockSpec(memory_space=pltpu.VMEM),
        compiler_params=params(),
        cost_estimate=cost(2e9, 2 * MIB),
        name="prefix",
    )(s)


def output_kernel(g_ref, s_ref, f_ref, c_ref, col_ref, y_ref, gate_ref, gain_ref, _, out_ref, held, state):
    group, core = g_ref[0], g_ref[1]

    @pl.when(pl.program_id(0) == 0)
    def _():
        for p in range(PAIRS):
            at = slice(p * LANES, (p + 1) * LANES)
            keep = jnp.where(core == 0, 1.0, edge_of(f_ref[p]))
            add = jnp.where(core == 0, 0.0, 1.0)
            for r in range(0, STATE, STRIP):
                rows = slice(r, r + STRIP)
                entering = keep * s_ref[p, rows].astype(F32) + add * f_ref[p, rows].astype(F32)
                state[rows, at] = entering.astype(BF16)

    rows = c_ref.shape[0]
    c = c_ref[...]
    grown = jnp.exp2(col_ref[:, 0:64])
    squares = jnp.zeros((rows, LANES), F32)
    for p in range(PAIRS):
        at = slice(p * LANES, (p + 1) * LANES)
        carried = jnp.dot(c, state[:, at], preferred_element_type=F32)
        factor = spread(grown, group * 32 + 2 * p, LANES)
        y = y_ref[:, at].astype(F32) + factor * carried
        gated = y * silu(gate_ref[:, at].astype(F32))
        squares = squares + gated * gated
        held[:, at] = gated
    mean = jnp.sum(squares, axis=1, keepdims=True) * (1.0 / GROUP_CHANNELS)
    scale = lax.rsqrt(mean + EPSILON)
    for p in range(PAIRS):
        at = slice(p * LANES, (p + 1) * LANES)
        out_ref[:, at] = (held[:, at] * scale * gain_ref[:, at].astype(F32)).astype(BF16)


def output_call(place, state, first, c, col, y, gate, gain, old):
    rows = 128
    whole = lambda n: pl.BlockSpec((PAIRS, n, 128), lambda i, g: (0, 0, 0))
    wide = pl.BlockSpec((rows, GROUP_CHANNELS), lambda i, g: (i, g[0]))
    in_specs = [
        whole(STATE),
        whole(SROWS),
        pl.BlockSpec((rows, STATE), lambda i, g: (i, 0)),
        pl.BlockSpec((rows, 128), lambda i, g: (i, 0)),
        pl.BlockSpec((rows, GROUP_CHANNELS), lambda i, g: (i, 0)),
        wide,
        pl.BlockSpec((1, GROUP_CHANNELS), lambda i, g: (0, g[0])),
    ]
    args = [place, state, first, c, col, y, gate, gain]
    if old is None:
        body = lambda *r: output_kernel(*r[:8], None, *r[8:])
        aliases = {}
    else:
        body = output_kernel
        in_specs.append(pl.BlockSpec(memory_space=pl.ANY))
        args.append(old)
        aliases = {8: 0}
    return pl.pallas_call(
        body,
        out_shape=jax.ShapeDtypeStruct((ROWS, 2 * GROUP_CHANNELS), BF16),
        grid_spec=pltpu.PrefetchScalarGridSpec(
            num_scalar_prefetch=1,
            grid=(ROWS // rows,),
            in_specs=in_specs,
            out_specs=wide,
            scratch_shapes=[
                pltpu.VMEM((rows, GROUP_CHANNELS), F32),
                pltpu.VMEM((STATE, GROUP_CHANNELS), BF16),
            ],
        ),
        input_output_aliases=aliases,
        compiler_params=params(),
        cost_estimate=cost(4e9, 5 * MIB),
        name="mixer_out",
    )(*args)


UNIT = 1024
SLOTS = 4
QPER = 8
SHARES = 6
SHARE_LANES = SLOTS * HDIM
SCALE = LOG2E * HDIM ** (-0.5)


GIVES = (14, 10)


def given(chip):
    return jnp.where(chip >= GIVES[0], 2, jnp.where(chip >= GIVES[1], 1, 0))


def attention_kernel(scal, own_ref, far_a, far_b, kv_hbm, out_ref, out_a, out_b, *scratch):
    kv, qs, acc, result, sem = scratch
    core, chip = scal[0], scal[1]
    cuts = sem.shape[0]
    length = kv.shape[0] // cuts
    copies = []
    for n in range(cuts):
        at = pl.ds(n * length, length)
        copies.append(pltpu.make_async_copy(kv_hbm.at[at], kv.at[at], sem.at[n]))
        copies[-1].start()
    for slot in range(SHARES * SLOTS):
        ref, h = own_ref, slot
        if slot >= 2 * QPER:
            ref, h = (far_a, far_b)[(slot - 2 * QPER) // SLOTS], slot % SLOTS
        hi, lo = split_hi_lo(ref[:, h * HDIM : (h + 1) * HDIM].astype(F32) * SCALE)
        qs[slot, :, 0:HDIM] = hi
        qs[slot, :, HDIM:] = lo
    for copy in copies:
        copy.wait()
    give, take = given(chip), given(CHIPS - 1 - chip)

    def share(j, carry):
        mirrored = j >= SHARES - 2
        its_chip = jnp.where(mirrored, CHIPS - 1 - chip, chip)
        its_core = jnp.where(mirrored, 1 - core, core)
        limit = its_chip // 2
        first_row = lax.rem(its_chip, 2) * (2 * ROWS) + its_core * ROWS
        used = jnp.where(
            j < 2, True, jnp.where(mirrored, take >= SHARES - j, give <= SHARES - 3 - j)
        )
        lane = jnp.where(j < 2, 0, HDIM)

        def scores_of(slot, keys):
            return lax.dot_general(
                qs[j * SLOTS + slot], keys, (((1,), (1,)), ((), ())), preferred_element_type=F32
            )

        def keys_values_of(u):
            rows = pl.ds(pl.multiple_of(u * UNIT, UNIT), UNIT)
            keys = kv[rows, pl.ds(pl.multiple_of(lane, HDIM), HDIM)]
            values = kv[rows, pl.ds(pl.multiple_of(2 * HDIM + lane, HDIM), HDIM)]
            keys = jnp.concatenate([keys, keys], 1)
            return keys, jnp.concatenate([values, jnp.ones((UNIT, HDIM), BF16)], 1)

        def visible_in(shift):
            row = lax.broadcasted_iota(jnp.int32, (ROWS, UNIT), 0) + first_row
            col = lax.broadcasted_iota(jnp.int32, (ROWS, UNIT), 1)
            return col + shift <= row

        def absorb(u, masked):
            keys, values = keys_values_of(u)
            scores = [scores_of(h, keys) for h in range(SLOTS)]
            for h in range(SLOTS):
                p = jnp.exp2(scores[h])
                if masked:
                    p = jnp.where(visible_in(0), p, 0.0)
                got = jnp.dot(p.astype(BF16), values, preferred_element_type=F32)
                acc[h] = got if masked else acc[h] + got

        @pl.when(used)
        def _():
            absorb(limit, True)

            def one(u, carry):
                absorb(u, False)
                return carry

            lax.fori_loop(0, limit, one, 0)
            least = jnp.full((ROWS, HDIM), 1.0, F32)
            most = jnp.full((ROWS, HDIM), 1.0, F32)
            for h in range(SLOTS):
                total = acc[h, :, HDIM:]
                least = jnp.minimum(least, total)
                most = jnp.maximum(most, total)
                result[j, :, h * HDIM : (h + 1) * HDIM] = (acc[h, :, :HDIM] / total).astype(BF16)
            safe = (jnp.min(least) > 2.0**-80) & (jnp.max(most) < 2.0**110)

            @pl.when(jnp.logical_not(safe))
            def _():
                def head(h, carry):
                    def unit_step(u, state):
                        top, total, summed = state
                        keys, values = keys_values_of(u)
                        shown = visible_in((u - limit) * UNIT)
                        scores = jnp.where(shown, scores_of(h, keys), -1e30)
                        new_top = jnp.maximum(top, jnp.max(scores, axis=1, keepdims=True))
                        shrink = jnp.exp2(top - new_top)
                        p = jnp.where(shown, jnp.exp2(scores - new_top), 0.0)
                        total = total * shrink + jnp.sum(p, axis=1, keepdims=True)
                        summed = summed * shrink + jnp.dot(
                            p.astype(BF16), values[:, :HDIM], preferred_element_type=F32
                        )
                        return new_top, total, summed

                    zero = jnp.zeros((ROWS, 1), F32)
                    state = (zero - 1e30, zero, jnp.zeros((ROWS, HDIM), F32))
                    _, total, summed = lax.fori_loop(0, limit + 1, unit_step, state)
                    at = pl.ds(pl.multiple_of(h * HDIM, HDIM), HDIM)
                    result[j, :, at] = (summed / total).astype(BF16)
                    return carry

                lax.fori_loop(0, SLOTS, head, 0)

        return carry

    lax.fori_loop(0, SHARES, share, 0)
    for j in range(SHARES):
        if j < SHARES - 2:
            out_ref[:, j * SHARE_LANES : (j + 1) * SHARE_LANES] = result[j]
    out_a[...] = result[SHARES - 2]
    out_b[...] = result[SHARES - 1]


def attention_call(scal, queries, far_a, far_b, kv):
    vmem = pl.BlockSpec(memory_space=pltpu.VMEM)
    return pl.pallas_call(
        attention_kernel,
        out_shape=(
            jax.ShapeDtypeStruct((ROWS, 2 * QPER * HDIM), BF16),
            jax.ShapeDtypeStruct((ROWS, SHARE_LANES), BF16),
            jax.ShapeDtypeStruct((ROWS, SHARE_LANES), BF16),
        ),
        in_specs=[
            pl.BlockSpec(memory_space=pltpu.SMEM),
            vmem,
            vmem,
            vmem,
            pl.BlockSpec(memory_space=pl.ANY),
        ],
        out_specs=(vmem, vmem, vmem),
        scratch_shapes=[
            pltpu.VMEM(kv.shape, BF16),
            pltpu.VMEM((SHARES * SLOTS, ROWS, 2 * HDIM), BF16),
            pltpu.VMEM((SLOTS, ROWS, 2 * HDIM), F32),
            pltpu.VMEM((SHARES, ROWS, SHARE_LANES), BF16),
            pltpu.SemaphoreType.DMA((4,)),
        ],
        compiler_params=params(32),
        cost_estimate=cost(3.2e10, 12 * MIB),
        name="attention",
    )(scal, queries, far_a, far_b, kv)


def permute(value, target):
    pairs = []
    for place in range(NY * NX * NCORE):
        y, x, c = place // (NX * NCORE), (place // NCORE) % NX, place % NCORE
        y, x, c = target(y, x, c)
        pairs.append((place, ((y % NY) * NX + x % NX) * NCORE + c))
    return lax.ppermute(value, "seq", pairs)


def swap(value):
    return permute(value, lambda y, x, c: (y, x, 1 - c))


ALL_CHIPS = [[chip * NCORE + core for chip in range(CHIPS)] for core in range(NCORE)]


def exchange(value):
    return lax.all_to_all(value, "seq", 0, 0, axis_index_groups=ALL_CHIPS, tiled=True)


def mirror(value, first_chip, to_low):
    seq = CHIPS * NCORE
    pairs = [(place, seq - 1 - place) for place in range(first_chip * NCORE, seq)]
    return lax.ppermute(value, "seq", pairs if to_low else [(low, high) for high, low in pairs])


def local(
    token_ids,
    token_tables,
    ssm_input,
    ssm_gate,
    ssm_bc,
    conv_input,
    conv_bc,
    skip_gain,
    norm_gain,
    queries,
    keys_values,
):
    place = lax.axis_index("seq")
    core = lax.rem(place, NCORE)
    chip = place // NCORE
    keep = core.reshape(1)

    kv = lax.all_gather(keys_values.reshape(ROWS, -1), "seq", axis=0, tiled=True)

    bc = ssm_bc.reshape(ROWS, -1)
    edge = jnp.concatenate([ssm_input[ROWS - 16 :], bc[ROWS - 16 :]], 1)
    seq = NY * NX * NCORE
    front = lax.ppermute(edge, "seq", [(i, i + 1) for i in range(seq - 1)])

    scal = jnp.stack([core, chip]).astype(jnp.int32)
    half = QPER * HDIM
    quarter = SHARE_LANES
    far_b = mirror(queries[:, half + quarter :], GIVES[1], True)
    far_a = mirror(queries[:, half : half + quarter], GIVES[0], True)

    row, col = table_call(token_ids, token_tables)
    taps_bc = conv_bc.reshape(CONV, -1)
    send = 1 - keep
    x_s, b_s, c_s, state_s = state_call(send, ssm_input, front, conv_input, bc, taps_bc, col)
    state_o = swap(state_s)
    col_k, far_b, far_a = lax.optimization_barrier((col, far_b, far_a))
    x_k, b_k, c_k, state_k = state_call(keep, ssm_input, front, conv_input, bc, taps_bc, col_k)
    joined = combine_call(keep, state_k, state_o)
    arrived = exchange(joined)
    y_s = inside_call(send, x_s, b_s, c_s, row, col, skip_gain)
    y_k = inside_call(keep, x_k, b_k, c_k, row, col, skip_gain)
    first_s = swap(state_k)
    arrived, y_k, y_s, first_s = lax.optimization_barrier((arrived, y_k, y_s, first_s))
    before = prefix_call(arrived)
    scal, before = lax.optimization_barrier((scal, before))
    entering_k = exchange(before)
    own, out_a, out_b = attention_call(scal, queries, far_a, far_b, kv)
    y_k, y_s, out_a, out_b, entering_k = lax.optimization_barrier(
        (y_k, y_s, out_a, out_b, entering_k)
    )
    entering_s = swap(entering_k)
    back_b, back_a = mirror(out_b, GIVES[1], False), mirror(out_a, GIVES[0], False)

    gain = norm_gain.reshape(1, -1)
    place_k = jnp.stack([core, core]).astype(jnp.int32)
    place_s = jnp.stack([1 - core, core]).astype(jnp.int32)
    mixed = output_call(place_k, entering_k, state_o, c_k, col, y_k, ssm_gate, gain, None)
    mixed = output_call(place_s, entering_s, first_s, c_s, col, y_s, ssm_gate, gain, mixed)
    give = given(chip)
    mixed, back_a, back_b = lax.optimization_barrier((mixed, back_a, back_b))
    attn = jnp.concatenate(
        [
            own[:, :half],
            jnp.where(give >= 2, back_a, own[:, half : half + quarter]),
            jnp.where(give >= 1, back_b, own[:, half + quarter :]),
        ],
        1,
    )
    return mixed, attn


def solution(mesh):
    in_specs = (
        P(("dp", "seq")),
        P(None, "head", None),
        P(("dp", "seq"), "head"),
        P(("dp", "seq"), "head"),
        P(("dp", "seq"), None, "head"),
        P(None, "head"),
        P(None, None, "head"),
        P("head"),
        P("head"),
        P(("dp", "seq"), "head"),
        P(("dp", "seq"), None, "head"),
    )
    out_specs = (P(("dp", "seq"), "head"), P(("dp", "seq"), "head"))
    return jax.shard_map(local, mesh=mesh, in_specs=in_specs, out_specs=out_specs, check_vma=False)
```

```python
import math

import jax
import jax.numpy as jnp
from jax import lax
from jax.experimental import pallas as pl
from jax.experimental.pallas import tpu as pltpu
from jax.sharding import PartitionSpec as P

MHDIM = 64
STATE = 256
CONV = 4
HDIM = 128
EPSILON = 1e-05
LOG2E = math.log2(math.e)
F32 = jnp.float32
BF16 = jnp.bfloat16

NY, NX, NCORE = 4, 4, 2
CHIPS = NY * NX
ROWS = 256
GROUP_CHANNELS = 2048
PAIRS = 16
EXTRA = 16
SROWS = STATE + EXTRA
MIB = 1 << 20


def params(mib=24):
    return pltpu.CompilerParams(vmem_limit_bytes=mib * MIB)


def cost(flops, nbytes, trans=0):
    return pl.CostEstimate(flops=int(flops), bytes_accessed=int(nbytes), transcendentals=int(trans))


def silu(v):
    half = 0.5 * v
    return half + half * jnp.tanh(half)


def split_hi_lo(v):
    hi = v.astype(BF16)
    lo = (v - hi.astype(F32)).astype(BF16)
    return hi, lo


def table_kernel(ids_ref, tab_ref, row_ref, col_ref, acc):
    step = pl.program_id(0)
    width = tab_ref.shape[2]

    @pl.when(step == 0)
    def _():
        acc[...] = jnp.zeros_like(acc)

    part = 1024
    for i in range(width // part):
        places = lax.broadcasted_iota(jnp.int32, (part, ROWS), 0) + (step * width + i * part)
        hot = jnp.where(places == ids_ref[...], 1.0, 0.0).astype(BF16)
        table = tab_ref[:, :, i * part : (i + 1) * part].reshape(128, part)
        acc[...] += jnp.dot(table, hot, preferred_element_type=F32)

    @pl.when(step == pl.num_programs(0) - 1)
    def _():
        u = lax.broadcasted_iota(jnp.int32, (ROWS, ROWS), 0)
        t = lax.broadcasted_iota(jnp.int32, (ROWS, ROWS), 1)
        tri = jnp.where(u <= t, 1.0, 0.0).astype(BF16)
        rate, raw = acc[0:64, :], acc[64:128, :]
        cum = jnp.dot(rate.astype(BF16), tri, preferred_element_type=F32) * (-LOG2E)
        size = jnp.maximum(raw, 0.0) + jnp.log1p(jnp.exp(-jnp.abs(raw)))
        both = jnp.concatenate([cum, cum - jnp.log(size) * LOG2E], 0)
        row_ref[...] = both
        col_ref[...] = both.T


def table_call(token_ids, token_tables):
    width = 4096
    return pl.pallas_call(
        table_kernel,
        out_shape=(
            jax.ShapeDtypeStruct((128, ROWS), F32),
            jax.ShapeDtypeStruct((ROWS, 128), F32),
        ),
        grid=(token_tables.shape[2] // width,),
        in_specs=[
            pl.BlockSpec((1, ROWS), lambda i: (0, 0)),
            pl.BlockSpec((2, 64, width), lambda i: (0, 0, i)),
        ],
        out_specs=[
            pl.BlockSpec((128, ROWS), lambda i: (0, 0)),
            pl.BlockSpec((ROWS, 128), lambda i: (0, 0)),
        ],
        scratch_shapes=[pltpu.VMEM((128, ROWS), F32)],
        compiler_params=params(),
        cost_estimate=cost(4e9, 2 * MIB),
        name="tables",
    )(token_ids.reshape(1, ROWS), token_tables)


def spread(values, first_head, width):
    hi, lo = split_hi_lo(values)
    r = lax.broadcasted_iota(jnp.int32, (64, width), 0)
    ch = lax.broadcasted_iota(jnp.int32, (64, width), 1)
    hot = jnp.where(r == first_head + ch // MHDIM, 1.0, 0.0).astype(BF16)
    return jnp.dot(
        jnp.concatenate([hi, lo], 1),
        jnp.concatenate([hot, hot], 0),
        preferred_element_type=F32,
    )


LANES = 128
STRIP = 64


def conv_strips(values_ref, front_ref, taps_ref, at, buffer, out_ref):
    buffer[0:16, :] = front_ref[:, at].astype(F32)
    for r in range(0, ROWS, STRIP):
        buffer[16 + r : 16 + r + STRIP, :] = values_ref[r : r + STRIP, at].astype(F32)
    taps = taps_ref[:, at].astype(F32)
    for r in range(0, ROWS, STRIP):
        total = taps[CONV - 1 : CONV] * buffer[16 + r : 16 + r + STRIP, :]
        for k in range(CONV - 1):
            total = total + taps[k : k + 1] * buffer[13 + k + r : 13 + k + r + STRIP, :]
        out_ref[r : r + STRIP, at] = silu(total).astype(BF16)


def state_kernel(group_ref, *refs):
    x_ref, xf_ref, xt_ref, b_ref, bf_ref, bt_ref, c_ref, cf_ref, ct_ref, col_ref = refs[:10]
    xc_ref, bc_ref, cc_ref, s_ref, buffer, scaled = refs[10:]
    group = group_ref[0]
    for i in range(STATE // LANES):
        at = slice(i * LANES, (i + 1) * LANES)
        conv_strips(b_ref, bf_ref, bt_ref, at, buffer.at[i], bc_ref)
        conv_strips(c_ref, cf_ref, ct_ref, at, buffer.at[2 + i], cc_ref)
    btrans = bc_ref[...].astype(F32).T.astype(BF16)
    last = col_ref[ROWS - 1 : ROWS, 0:64]
    tail = jnp.exp2(last - col_ref[:, 64:128])
    weights = jnp.concatenate([tail, jnp.broadcast_to(jnp.exp2(last), (EXTRA, 64))], 0)
    place = lax.broadcasted_iota(jnp.int32, (EXTRA, LANES), 0)
    for p in range(PAIRS):
        at = slice(p * LANES, (p + 1) * LANES)
        conv_strips(x_ref, xf_ref, xt_ref, at, buffer.at[p % 4], xc_ref)
        wide = spread(weights, group * 32 + 2 * p, LANES)
        for r in range(0, ROWS, STRIP):
            rows = slice(r, r + STRIP)
            scaled[p % 4, rows, :] = (xc_ref[rows, at].astype(F32) * wide[rows]).astype(BF16)
        state = jnp.dot(btrans, scaled[p % 4], preferred_element_type=F32)
        s_ref[p, 0:STATE, :] = state.astype(BF16)
        hi, lo = split_hi_lo(wide[ROWS:])
        edge = jnp.where(place == 0, hi.astype(F32), jnp.where(place == 1, lo.astype(F32), 0.0))
        s_ref[p, STATE:SROWS, :] = edge.astype(BF16)


def state_call(group, ssm_input, front, conv_input, bc, conv_bc, col):
    wide = lambda rows: pl.BlockSpec((rows, GROUP_CHANNELS), lambda j, g: (0, g[0]))
    narrow = lambda rows, base: pl.BlockSpec((rows, STATE), lambda j, g: (0, base + g[0]))
    whole = lambda shape: pl.BlockSpec(shape, lambda j, g: (0,) * len(shape))
    shapes = ((ROWS, GROUP_CHANNELS), (ROWS, STATE), (ROWS, STATE), (PAIRS, SROWS, 128))
    return pl.pallas_call(
        state_kernel,
        out_shape=tuple(jax.ShapeDtypeStruct(shape, BF16) for shape in shapes),
        grid_spec=pltpu.PrefetchScalarGridSpec(
            num_scalar_prefetch=1,
            grid=(1,),
            in_specs=[
                wide(ROWS),
                wide(16),
                wide(CONV),
                narrow(ROWS, 0),
                narrow(16, 16),
                narrow(CONV, 0),
                narrow(ROWS, 2),
                narrow(16, 18),
                narrow(CONV, 2),
                whole((ROWS, 128)),
            ],
            out_specs=[whole(shape) for shape in shapes],
            scratch_shapes=[
                pltpu.VMEM((4, 16 + ROWS, LANES), F32),
                pltpu.VMEM((4, ROWS, LANES), BF16),
            ],
        ),
        compiler_params=params(),
        cost_estimate=cost(4e9, 3 * MIB),
        name="conv_state",
    )(group, ssm_input, front, conv_input, bc, front, conv_bc, bc, front, conv_bc, col)


def inside_kernel(g_ref, x_ref, b_ref, c_ref, row_ref, col_ref, skip_ref, y_ref, gram, held):
    g = g_ref[0]
    half = ROWS // 2
    product = lax.dot_general(
        c_ref[...], b_ref[...], (((1,), (1,)), ((), ())), preferred_element_type=F32
    )
    t = lax.broadcasted_iota(jnp.int32, (ROWS, ROWS), 0)
    s = lax.broadcasted_iota(jnp.int32, (ROWS, ROWS), 1)
    gram[...] = jnp.where(s <= t, product, 0.0)
    columns = pltpu.roll(col_ref[...], lax.rem(128 - g * 32, 128), 1)
    lane = lax.broadcasted_iota(jnp.int32, (half, LANES), 1)
    for p in range(PAIRS):
        at = slice(p * LANES, (p + 1) * LANES)
        for i in range(2):
            h = 2 * p + i
            entries = row_ref[pl.ds(64 + g * 32 + h, 1), :]
            slot = held.at[2 * (p % 2) + i]
            for r in range(0, ROWS, STRIP):
                width = half if r < half else ROWS
                power = columns[r : r + STRIP, h : h + 1] - entries[:, :width]
                weight = gram[r : r + STRIP, :width] * jnp.exp2(jnp.minimum(power, 1.0))
                slot[r : r + STRIP, :width] = weight.astype(BF16)
        head = g * 32 + 2 * p
        skip = jnp.where(lane[0:1] < MHDIM, skip_ref[head], skip_ref[head + 1])
        for r, width in ((0, half), (half, ROWS)):
            first, second = (
                jnp.dot(
                    held[2 * (p % 2) + i, r : r + half, :width],
                    x_ref[:width, at],
                    preferred_element_type=F32,
                )
                for i in range(2)
            )
            rows = slice(r, r + half)
            y = jnp.where(lane < MHDIM, first, second) + skip * x_ref[rows, at].astype(F32)
            y_ref[rows, at] = y.astype(BF16)


def inside_call(group, x, b, c, row, col, skip):
    vmem = pl.BlockSpec(memory_space=pltpu.VMEM)
    smem = pl.BlockSpec(memory_space=pltpu.SMEM)
    return pl.pallas_call(
        inside_kernel,
        out_shape=jax.ShapeDtypeStruct((ROWS, GROUP_CHANNELS), BF16),
        in_specs=[smem, vmem, vmem, vmem, vmem, vmem, smem],
        out_specs=vmem,
        scratch_shapes=[pltpu.VMEM((ROWS, ROWS), F32), pltpu.VMEM((4, ROWS, ROWS), BF16)],
        compiler_params=params(),
        cost_estimate=cost(5e9, 3 * MIB),
        name="inside",
    )(group, x, b, c, row, col, skip)


def edge_of(s):
    return s[STATE : STATE + 1, :].astype(F32) + s[STATE + 1 : STATE + 2, :].astype(F32)


def combine_kernel(core_ref, own_ref, other_ref, out_ref):
    own_first = core_ref[0] == 0
    place = lax.broadcasted_iota(jnp.int32, (EXTRA, 128), 0)
    for p in range(PAIRS):
        own_edge, other_edge = edge_of(own_ref[p]), edge_of(other_ref[p])
        keep_own = jnp.where(own_first, other_edge, 1.0)
        keep_other = jnp.where(own_first, 1.0, own_edge)
        for r in range(0, STATE, STRIP):
            rows = slice(r, r + STRIP)
            own, other = own_ref[p, rows].astype(F32), other_ref[p, rows].astype(F32)
            out_ref[p, rows, :] = (keep_own * own + keep_other * other).astype(BF16)
        hi, lo = split_hi_lo(own_edge * other_edge)
        out_ref[p, STATE:SROWS, :] = jnp.where(
            place == 0, hi.astype(F32), jnp.where(place == 1, lo.astype(F32), 0.0)
        ).astype(BF16)


def combine_call(core, own, other):
    vmem = pl.BlockSpec(memory_space=pltpu.VMEM)
    return pl.pallas_call(
        combine_kernel,
        out_shape=jax.ShapeDtypeStruct((PAIRS, SROWS, 128), BF16),
        in_specs=[pl.BlockSpec(memory_space=pltpu.SMEM), vmem, vmem],
        out_specs=vmem,
        compiler_params=params(),
        cost_estimate=cost(2e9, 3 * MIB),
        name="combine",
    )(core, own, other)


def prefix_kernel(s_ref, out_ref):
    carried = jnp.zeros((STATE, 128), F32)
    for k in range(CHIPS):
        out_ref[k] = carried.astype(BF16)
        if k < CHIPS - 1:
            s = s_ref[k].astype(F32)
            carried = edge_of(s_ref[k]) * carried + s[:STATE]


def prefix_call(s):
    return pl.pallas_call(
        prefix_kernel,
        out_shape=jax.ShapeDtypeStruct((CHIPS, STATE, 128), BF16),
        in_specs=[pl.BlockSpec(memory_space=pltpu.VMEM)],
        out_specs=pl.BlockSpec(memory_space=pltpu.VMEM),
        compiler_params=params(),
        cost_estimate=cost(2e9, 2 * MIB),
        name="prefix",
    )(s)


def output_kernel(g_ref, s_ref, f_ref, c_ref, col_ref, y_ref, gate_ref, gain_ref, _, out_ref, held, state):
    group, core = g_ref[0], g_ref[1]

    @pl.when(pl.program_id(0) == 0)
    def _():
        for p in range(PAIRS):
            at = slice(p * LANES, (p + 1) * LANES)
            keep = jnp.where(core == 0, 1.0, edge_of(f_ref[p]))
            add = jnp.where(core == 0, 0.0, 1.0)
            for r in range(0, STATE, STRIP):
                rows = slice(r, r + STRIP)
                entering = keep * s_ref[p, rows].astype(F32) + add * f_ref[p, rows].astype(F32)
                state[rows, at] = entering.astype(BF16)

    rows = c_ref.shape[0]
    c = c_ref[...]
    grown = jnp.exp2(col_ref[:, 0:64])
    squares = jnp.zeros((rows, LANES), F32)
    for p in range(PAIRS):
        at = slice(p * LANES, (p + 1) * LANES)
        carried = jnp.dot(c, state[:, at], preferred_element_type=F32)
        factor = spread(grown, group * 32 + 2 * p, LANES)
        y = y_ref[:, at].astype(F32) + factor * carried
        gated = y * silu(gate_ref[:, at].astype(F32))
        squares = squares + gated * gated
        held[:, at] = gated
    mean = jnp.sum(squares, axis=1, keepdims=True) * (1.0 / GROUP_CHANNELS)
    scale = lax.rsqrt(mean + EPSILON)
    for p in range(PAIRS):
        at = slice(p * LANES, (p + 1) * LANES)
        out_ref[:, at] = (held[:, at] * scale * gain_ref[:, at].astype(F32)).astype(BF16)


def output_call(place, state, first, c, col, y, gate, gain, old):
    rows = 128
    whole = lambda n: pl.BlockSpec((PAIRS, n, 128), lambda i, g: (0, 0, 0))
    wide = pl.BlockSpec((rows, GROUP_CHANNELS), lambda i, g: (i, g[0]))
    in_specs = [
        whole(STATE),
        whole(SROWS),
        pl.BlockSpec((rows, STATE), lambda i, g: (i, 0)),
        pl.BlockSpec((rows, 128), lambda i, g: (i, 0)),
        pl.BlockSpec((rows, GROUP_CHANNELS), lambda i, g: (i, 0)),
        wide,
        pl.BlockSpec((1, GROUP_CHANNELS), lambda i, g: (0, g[0])),
    ]
    args = [place, state, first, c, col, y, gate, gain]
    if old is None:
        body = lambda *r: output_kernel(*r[:8], None, *r[8:])
        aliases = {}
    else:
        body = output_kernel
        in_specs.append(pl.BlockSpec(memory_space=pl.ANY))
        args.append(old)
        aliases = {8: 0}
    return pl.pallas_call(
        body,
        out_shape=jax.ShapeDtypeStruct((ROWS, 2 * GROUP_CHANNELS), BF16),
        grid_spec=pltpu.PrefetchScalarGridSpec(
            num_scalar_prefetch=1,
            grid=(ROWS // rows,),
            in_specs=in_specs,
            out_specs=wide,
            scratch_shapes=[
                pltpu.VMEM((rows, GROUP_CHANNELS), F32),
                pltpu.VMEM((STATE, GROUP_CHANNELS), BF16),
            ],
        ),
        input_output_aliases=aliases,
        compiler_params=params(),
        cost_estimate=cost(4e9, 5 * MIB),
        name="mixer_out",
    )(*args)


UNIT = 1024
SLOTS = 4
QPER = 8
SHARE_LANES = SLOTS * HDIM
SCALE = LOG2E * HDIM ** (-0.5)
OFFSETS = (0, -1, 1, 2)
HALF = QPER * HDIM


def given(chip):
    return jnp.where(chip >= 14, 2, jnp.where(chip >= 10, 1, 0))


def attention_kernel(kinds, pieces, scal, *refs):
    queries = refs[: len(kinds)]
    kv_refs = refs[len(kinds) : len(kinds) + pieces]
    outs = refs[len(kinds) + pieces : -5]
    kv, qs, acc, result, sem = refs[-5:]
    core, chip = scal[0], scal[1]
    y, x = chip // NX, lax.rem(chip, NX)
    rows_of_chip = NCORE * ROWS
    copies = []
    for n in range(CHIPS):
        two, one = OFFSETS[n // NX], OFFSETS[n % NX]
        dy, dx = jnp.where(core == 0, two, one), jnp.where(core == 0, one, two)
        unit = lax.rem(y + dy + NY, NY) * NX + lax.rem(x + dx + NX, NX)
        source = kv_refs[n // 2].at[pl.ds((n % 2) * rows_of_chip, rows_of_chip)]
        to = pl.ds(pl.multiple_of(unit * rows_of_chip, rows_of_chip), rows_of_chip)
        copies.append(pltpu.make_async_copy(source, kv.at[to], sem.at[n]))
        copies[-1].start()
    for n, ref in enumerate(queries):
        for h in range(QPER):
            at = pl.ds(h * HDIM, HDIM)
            if kinds[n] == "own":
                at = pl.ds(pl.multiple_of(core * HALF + h * HDIM, HDIM), HDIM)
            hi, lo = split_hi_lo(ref[:, at].astype(F32) * SCALE)
            qs[n * QPER + h, :, 0:HDIM] = hi
            qs[n * QPER + h, :, HDIM:] = lo
    for copy in copies:
        copy.wait()
    give, take = given(chip), given(CHIPS - 1 - chip)
    shares = 2 * len(kinds)

    def share(j, carry):
        kind = j // 2
        second = lax.rem(j, 2)
        far = kind == 2
        its_chip = jnp.where(far, CHIPS - 1 - chip, chip)
        its_core = jnp.where(kind == 0, core, 1 - core)
        used = jnp.where(
            kind == 0, True, jnp.where(far, take >= 2 - second, give <= 1 - second)
        )
        limit = its_chip // 2
        first_row = lax.rem(its_chip, 2) * rows_of_chip + its_core * ROWS

        def scores_of(slot, keys):
            return lax.dot_general(
                qs[j * SLOTS + slot], keys, (((1,), (1,)), ((), ())), preferred_element_type=F32
            )

        def keys_values_of(u):
            rows = pl.ds(pl.multiple_of(u * UNIT, UNIT), UNIT)
            keys, values = kv[rows, 0:HDIM], kv[rows, HDIM:]
            keys = jnp.concatenate([keys, keys], 1)
            return keys, jnp.concatenate([values, jnp.ones((UNIT, HDIM), BF16)], 1)

        def visible_in(shift):
            row = lax.broadcasted_iota(jnp.int32, (ROWS, UNIT), 0) + first_row
            col = lax.broadcasted_iota(jnp.int32, (ROWS, UNIT), 1)
            return col + shift <= row

        def absorb(u, masked):
            keys, values = keys_values_of(u)
            scores = [scores_of(h, keys) for h in range(SLOTS)]
            for h in range(SLOTS):
                p = jnp.exp2(scores[h])
                if masked:
                    p = jnp.where(visible_in(0), p, 0.0)
                got = jnp.dot(p.astype(BF16), values, preferred_element_type=F32)
                acc[h] = got if masked else acc[h] + got

        @pl.when(used)
        def _():
            absorb(limit, True)

            def one(u, carry):
                absorb(u, False)
                return carry

            lax.fori_loop(0, limit, one, 0)
            least = jnp.full((ROWS, HDIM), 1.0, F32)
            most = jnp.full((ROWS, HDIM), 1.0, F32)
            for h in range(SLOTS):
                total = acc[h, :, HDIM:]
                least = jnp.minimum(least, total)
                most = jnp.maximum(most, total)
                result[j, :, h * HDIM : (h + 1) * HDIM] = (acc[h, :, :HDIM] / total).astype(BF16)
            safe = (jnp.min(least) > 2.0**-80) & (jnp.max(most) < 2.0**110)

            @pl.when(jnp.logical_not(safe))
            def _():
                def head(h, carry):
                    def unit_step(u, state):
                        top, total, summed = state
                        keys, values = keys_values_of(u)
                        shown = visible_in((u - limit) * UNIT)
                        scores = jnp.where(shown, scores_of(h, keys), -1e30)
                        new_top = jnp.maximum(top, jnp.max(scores, axis=1, keepdims=True))
                        shrink = jnp.exp2(top - new_top)
                        p = jnp.where(shown, jnp.exp2(scores - new_top), 0.0)
                        total = total * shrink + jnp.sum(p, axis=1, keepdims=True)
                        summed = summed * shrink + jnp.dot(
                            p.astype(BF16), values[:, :HDIM], preferred_element_type=F32
                        )
                        return new_top, total, summed

                    zero = jnp.zeros((ROWS, 1), F32)
                    state = (zero - 1e30, zero, jnp.zeros((ROWS, HDIM), F32))
                    _, total, summed = lax.fori_loop(0, limit + 1, unit_step, state)
                    at = pl.ds(pl.multiple_of(h * HDIM, HDIM), HDIM)
                    result[j, :, at] = (summed / total).astype(BF16)
                    return carry

                lax.fori_loop(0, SLOTS, head, 0)

        return carry

    lax.fori_loop(0, shares, share, 0)
    for j in range(shares):
        outs[j // 2][:, (j % 2) * SHARE_LANES : (j % 2 + 1) * SHARE_LANES] = result[j]


def attention_call(scal, kinds, queries, pieces):
    vmem = pl.BlockSpec(memory_space=pltpu.VMEM)
    slots = QPER * len(kinds)

    def body(*refs):
        attention_kernel(kinds, len(pieces), *refs)

    return pl.pallas_call(
        body,
        out_shape=tuple(jax.ShapeDtypeStruct((ROWS, HALF), BF16) for _ in kinds),
        in_specs=[pl.BlockSpec(memory_space=pltpu.SMEM)]
        + [vmem] * len(kinds)
        + [pl.BlockSpec(memory_space=pl.ANY)] * len(pieces),
        out_specs=tuple(vmem for _ in kinds),
        scratch_shapes=[
            pltpu.VMEM((CHIPS * NCORE * ROWS, 2 * HDIM), BF16),
            pltpu.VMEM((slots, ROWS, 2 * HDIM), BF16),
            pltpu.VMEM((SLOTS, ROWS, 2 * HDIM), F32),
            pltpu.VMEM((2 * len(kinds), ROWS, SHARE_LANES), BF16),
            pltpu.SemaphoreType.DMA((CHIPS,)),
        ],
        compiler_params=params(58),
        cost_estimate=cost(3e10, 8 * MIB),
        name="attention",
    )(scal, *queries, *pieces)


def join_kernel(first, second, third, fourth, front_ref, back_ref):
    rows = first.shape[0]
    front_ref[0:rows] = first[...]
    front_ref[rows:] = second[...]
    back_ref[0:rows] = third[...]
    back_ref[rows:] = fourth[...]


def join_call(*parts):
    vmem = pl.BlockSpec(memory_space=pltpu.VMEM)
    rows, width = parts[0].shape
    return pl.pallas_call(
        join_kernel,
        out_shape=(jax.ShapeDtypeStruct((2 * rows, width), BF16),) * 2,
        in_specs=[vmem] * 4,
        out_specs=(vmem, vmem),
        compiler_params=params(),
        cost_estimate=cost(1e9, 2 * MIB),
        name="join",
    )(*parts)


def permute(value, target):
    pairs = []
    for place in range(NY * NX * NCORE):
        y, x, c = place // (NX * NCORE), (place // NCORE) % NX, place % NCORE
        y, x, c = target(y, x, c)
        pairs.append((place, ((y % NY) * NX + x % NX) * NCORE + c))
    return lax.ppermute(value, "seq", pairs)


def swap(value):
    return permute(value, lambda y, x, c: (y, x, 1 - c))


def along(value, step, second):
    def target(y, x, c):
        return (y, x + step, c) if c == second else (y + step, x, c)

    return permute(value, target)


ALL_CHIPS = [[chip * NCORE + core for chip in range(CHIPS)] for core in range(NCORE)]


def exchange(value):
    return lax.all_to_all(value, "seq", 0, 0, axis_index_groups=ALL_CHIPS, tiled=True)


def mirror(value, to_low):
    seq = CHIPS * NCORE
    pairs = [(place, seq - 1 - place) for place in range(10 * NCORE, seq)]
    return lax.ppermute(value, "seq", pairs if to_low else [(low, high) for high, low in pairs])


def local(
    token_ids,
    token_tables,
    ssm_input,
    ssm_gate,
    ssm_bc,
    conv_input,
    conv_bc,
    skip_gain,
    norm_gain,
    queries,
    keys_values,
):
    place = lax.axis_index("seq")
    core = lax.rem(place, NCORE)
    chip = place // NCORE
    keep = core.reshape(1)

    kv = keys_values.reshape(ROWS, 4, HDIM)
    zero = jnp.concatenate([kv[:, 0], kv[:, 2]], 1)
    one = jnp.concatenate([kv[:, 1], kv[:, 3]], 1)
    mine = jnp.where(core == 0, zero, one)
    from_other = swap(jnp.where(core == 0, one, zero))

    bc = ssm_bc.reshape(ROWS, -1)
    edge = jnp.concatenate([ssm_input[ROWS - 16 :], bc[ROWS - 16 :]], 1)
    seq = NY * NX * NCORE
    front = lax.ppermute(edge, "seq", [(i, i + 1) for i in range(seq - 1)])

    scal = jnp.stack([core, chip]).astype(jnp.int32)
    together = lax.optimization_barrier

    query_other = lax.dynamic_slice_in_dim(queries, (1 - core) * HALF, HALF, 1)
    near = swap(query_other)
    far = mirror(query_other, True)
    row, col = table_call(token_ids, token_tables)
    from_other, row, col = together((from_other, row, col))
    unit = jnp.where(
        core == 0,
        jnp.concatenate([mine, from_other], 0),
        jnp.concatenate([from_other, mine], 0),
    )
    left, right, across = (along(unit, step, 0) for step in (1, -1, 2))
    taps_bc = conv_bc.reshape(CONV, -1)
    send = 1 - keep
    x_s, b_s, c_s, state_s = state_call(send, ssm_input, front, conv_input, bc, taps_bc, col)
    state_o = swap(state_s)
    left, right, across, x_s = together((left, right, across, x_s))
    line_a, line_b = join_call(unit, left, right, across)
    left_a, right_b = along(line_a, 1, 1), along(line_b, -1, 1)
    left_b, right_a = along(line_b, 1, 1), along(line_a, -1, 1)
    line_a, line_b, col_k = together((line_a, line_b, col))
    x_k, b_k, c_k, state_k = state_call(keep, ssm_input, front, conv_input, bc, taps_bc, col_k)
    joined = combine_call(keep, state_k, state_o)
    left_a, right_b, left_b, right_a, joined, near, far = together(
        (left_a, right_b, left_b, right_a, joined, near, far)
    )
    across_a, across_b = along(left_a, 1, 1), along(right_b, -1, 1)
    joined, x_s, x_k = together((joined, x_s, x_k))
    arrived = exchange(joined)
    y_s = inside_call(send, x_s, b_s, c_s, row, col, skip_gain)
    y_k = inside_call(keep, x_k, b_k, c_k, row, col, skip_gain)
    pieces = [line_a, line_b, left_a, left_b, right_a, right_b, across_a, across_b]
    arrived, y_k, y_s, state_k = together((arrived, y_k, y_s, state_k))
    first_s = swap(state_k)
    before = prefix_call(arrived)
    entering_k = exchange(before)
    scal, before = together((scal, before))
    own, near_out, far_out = attention_call(
        scal, ("own", "near", "far"), [queries, near, far], pieces
    )
    y_k, y_s, far_out, near_out, entering_k = together((y_k, y_s, far_out, near_out, entering_k))
    entering_s = swap(entering_k)
    back, near_back = mirror(far_out, False), swap(near_out)

    gain = norm_gain.reshape(1, -1)
    place_k = jnp.stack([core, core]).astype(jnp.int32)
    place_s = jnp.stack([1 - core, core]).astype(jnp.int32)
    mixed = output_call(place_k, entering_k, state_o, c_k, col, y_k, ssm_gate, gain, None)
    mixed = output_call(place_s, entering_s, first_s, c_s, col, y_s, ssm_gate, gain, mixed)
    give = given(chip)
    mixed, back, near_back = together((mixed, back, near_back))
    other = jnp.concatenate(
        [
            jnp.where(give >= 2, back[:, :SHARE_LANES], near_back[:, :SHARE_LANES]),
            jnp.where(give >= 1, back[:, SHARE_LANES:], near_back[:, SHARE_LANES:]),
        ],
        1,
    )
    attn = jnp.where(
        core == 0, jnp.concatenate([own, other], 1), jnp.concatenate([other, own], 1)
    )
    return mixed, attn


def solution(mesh):
    in_specs = (
        P(("dp", "seq")),
        P(None, "head", None),
        P(("dp", "seq"), "head"),
        P(("dp", "seq"), "head"),
        P(("dp", "seq"), None, "head"),
        P(None, "head"),
        P(None, None, "head"),
        P("head"),
        P("head"),
        P(("dp", "seq"), "head"),
        P(("dp", "seq"), None, "head"),
    )
    out_specs = (P(("dp", "seq"), "head"), P(("dp", "seq"), "head"))
    return jax.shard_map(local, mesh=mesh, in_specs=in_specs, out_specs=out_specs, check_vma=False)
```

```python
import math

import jax
import jax.numpy as jnp
from jax import lax
from jax.experimental import pallas as pl
from jax.experimental.pallas import tpu as pltpu
from jax.sharding import PartitionSpec as P

MHDIM = 64
STATE = 256
CONV = 4
HDIM = 128
EPSILON = 1e-05
LOG2E = math.log2(math.e)
F32 = jnp.float32
BF16 = jnp.bfloat16

NY, NX, NCORE = 4, 4, 2
CHIPS = NY * NX
ROWS = 256
GROUP_CHANNELS = 2048
PAIRS = 16
EXTRA = 16
SROWS = STATE + EXTRA
MIB = 1 << 20


def params(mib=24):
    return pltpu.CompilerParams(vmem_limit_bytes=mib * MIB)


def cost(flops, nbytes, trans=0):
    return pl.CostEstimate(flops=int(flops), bytes_accessed=int(nbytes), transcendentals=int(trans))


def silu(v):
    half = 0.5 * v
    return half + half * jnp.tanh(half)


def split_hi_lo(v):
    hi = v.astype(BF16)
    lo = (v - hi.astype(F32)).astype(BF16)
    return hi, lo


def table_kernel(ids_ref, tab_ref, row_ref, col_ref, acc):
    step = pl.program_id(0)
    width = tab_ref.shape[2]

    @pl.when(step == 0)
    def _():
        acc[...] = jnp.zeros_like(acc)

    part = 1024
    for i in range(width // part):
        places = lax.broadcasted_iota(jnp.int32, (part, ROWS), 0) + (step * width + i * part)
        hot = jnp.where(places == ids_ref[...], 1.0, 0.0).astype(BF16)
        table = tab_ref[:, :, i * part : (i + 1) * part].reshape(128, part)
        acc[...] += jnp.dot(table, hot, preferred_element_type=F32)

    @pl.when(step == pl.num_programs(0) - 1)
    def _():
        u = lax.broadcasted_iota(jnp.int32, (ROWS, ROWS), 0)
        t = lax.broadcasted_iota(jnp.int32, (ROWS, ROWS), 1)
        tri = jnp.where(u <= t, 1.0, 0.0).astype(BF16)
        rate, raw = acc[0:64, :], acc[64:128, :]
        cum = jnp.dot(rate.astype(BF16), tri, preferred_element_type=F32) * (-LOG2E)
        size = jnp.maximum(raw, 0.0) + jnp.log1p(jnp.exp(-jnp.abs(raw)))
        both = jnp.concatenate([cum, cum - jnp.log(size) * LOG2E], 0)
        row_ref[...] = both
        col_ref[...] = both.T


def table_call(token_ids, token_tables):
    width = 4096
    return pl.pallas_call(
        table_kernel,
        out_shape=(
            jax.ShapeDtypeStruct((128, ROWS), F32),
            jax.ShapeDtypeStruct((ROWS, 128), F32),
        ),
        grid=(token_tables.shape[2] // width,),
        in_specs=[
            pl.BlockSpec((1, ROWS), lambda i: (0, 0)),
            pl.BlockSpec((2, 64, width), lambda i: (0, 0, i)),
        ],
        out_specs=[
            pl.BlockSpec((128, ROWS), lambda i: (0, 0)),
            pl.BlockSpec((ROWS, 128), lambda i: (0, 0)),
        ],
        scratch_shapes=[pltpu.VMEM((128, ROWS), F32)],
        compiler_params=params(),
        cost_estimate=cost(4e9, 2 * MIB),
        name="tables",
    )(token_ids.reshape(1, ROWS), token_tables)


def spread(values, first_head, width):
    hi, lo = split_hi_lo(values)
    r = lax.broadcasted_iota(jnp.int32, (64, width), 0)
    ch = lax.broadcasted_iota(jnp.int32, (64, width), 1)
    hot = jnp.where(r == first_head + ch // MHDIM, 1.0, 0.0).astype(BF16)
    return jnp.dot(
        jnp.concatenate([hi, lo], 1),
        jnp.concatenate([hot, hot], 0),
        preferred_element_type=F32,
    )


LANES = 128
STRIP = 64


def conv_strips(values_ref, front_ref, taps_ref, at, buffer, out_ref):
    buffer[0:16, :] = front_ref[:, at].astype(F32)
    for r in range(0, ROWS, STRIP):
        buffer[16 + r : 16 + r + STRIP, :] = values_ref[r : r + STRIP, at].astype(F32)
    taps = taps_ref[:, at].astype(F32)
    for r in range(0, ROWS, STRIP):
        total = taps[CONV - 1 : CONV] * buffer[16 + r : 16 + r + STRIP, :]
        for k in range(CONV - 1):
            total = total + taps[k : k + 1] * buffer[13 + k + r : 13 + k + r + STRIP, :]
        out_ref[r : r + STRIP, at] = silu(total).astype(BF16)


def state_kernel(group_ref, *refs):
    x_ref, xf_ref, xt_ref, b_ref, bf_ref, bt_ref, c_ref, cf_ref, ct_ref, col_ref = refs[:10]
    xc_ref, bc_ref, cc_ref, s_ref, buffer, scaled = refs[10:]
    group = group_ref[0]
    for i in range(STATE // LANES):
        at = slice(i * LANES, (i + 1) * LANES)
        conv_strips(b_ref, bf_ref, bt_ref, at, buffer.at[i], bc_ref)
        conv_strips(c_ref, cf_ref, ct_ref, at, buffer.at[2 + i], cc_ref)
    btrans = bc_ref[...].astype(F32).T.astype(BF16)
    last = col_ref[ROWS - 1 : ROWS, 0:64]
    tail = jnp.exp2(last - col_ref[:, 64:128])
    weights = jnp.concatenate([tail, jnp.broadcast_to(jnp.exp2(last), (EXTRA, 64))], 0)
    place = lax.broadcasted_iota(jnp.int32, (EXTRA, LANES), 0)
    for p in range(PAIRS):
        at = slice(p * LANES, (p + 1) * LANES)
        conv_strips(x_ref, xf_ref, xt_ref, at, buffer.at[p % 4], xc_ref)
        wide = spread(weights, group * 32 + 2 * p, LANES)
        for r in range(0, ROWS, STRIP):
            rows = slice(r, r + STRIP)
            scaled[p % 4, rows, :] = (xc_ref[rows, at].astype(F32) * wide[rows]).astype(BF16)
        state = jnp.dot(btrans, scaled[p % 4], preferred_element_type=F32)
        s_ref[p, 0:STATE, :] = state.astype(BF16)
        hi, lo = split_hi_lo(wide[ROWS:])
        edge = jnp.where(place == 0, hi.astype(F32), jnp.where(place == 1, lo.astype(F32), 0.0))
        s_ref[p, STATE:SROWS, :] = edge.astype(BF16)


def state_call(group, ssm_input, front, conv_input, bc, conv_bc, col):
    wide = lambda rows: pl.BlockSpec((rows, GROUP_CHANNELS), lambda j, g: (0, g[0]))
    narrow = lambda rows, base: pl.BlockSpec((rows, STATE), lambda j, g: (0, base + g[0]))
    whole = lambda shape: pl.BlockSpec(shape, lambda j, g: (0,) * len(shape))
    shapes = ((ROWS, GROUP_CHANNELS), (ROWS, STATE), (ROWS, STATE), (PAIRS, SROWS, 128))
    return pl.pallas_call(
        state_kernel,
        out_shape=tuple(jax.ShapeDtypeStruct(shape, BF16) for shape in shapes),
        grid_spec=pltpu.PrefetchScalarGridSpec(
            num_scalar_prefetch=1,
            grid=(1,),
            in_specs=[
                wide(ROWS),
                wide(16),
                wide(CONV),
                narrow(ROWS, 0),
                narrow(16, 16),
                narrow(CONV, 0),
                narrow(ROWS, 2),
                narrow(16, 18),
                narrow(CONV, 2),
                whole((ROWS, 128)),
            ],
            out_specs=[whole(shape) for shape in shapes],
            scratch_shapes=[
                pltpu.VMEM((4, 16 + ROWS, LANES), F32),
                pltpu.VMEM((4, ROWS, LANES), BF16),
            ],
        ),
        compiler_params=params(),
        cost_estimate=cost(4e9, 3 * MIB),
        name="conv_state",
    )(group, ssm_input, front, conv_input, bc, front, conv_bc, bc, front, conv_bc, col)


def inside_kernel(g_ref, x_ref, b_ref, c_ref, row_ref, col_ref, skip_ref, y_ref, gram, held):
    g = g_ref[0]
    half = ROWS // 2
    product = lax.dot_general(
        c_ref[...], b_ref[...], (((1,), (1,)), ((), ())), preferred_element_type=F32
    )
    t = lax.broadcasted_iota(jnp.int32, (ROWS, ROWS), 0)
    s = lax.broadcasted_iota(jnp.int32, (ROWS, ROWS), 1)
    gram[...] = jnp.where(s <= t, product, 0.0)
    columns = pltpu.roll(col_ref[...], lax.rem(128 - g * 32, 128), 1)
    lane = lax.broadcasted_iota(jnp.int32, (half, LANES), 1)
    for p in range(PAIRS):
        at = slice(p * LANES, (p + 1) * LANES)
        for i in range(2):
            h = 2 * p + i
            entries = row_ref[pl.ds(64 + g * 32 + h, 1), :]
            slot = held.at[2 * (p % 2) + i]
            for r in range(0, ROWS, STRIP):
                width = half if r < half else ROWS
                power = columns[r : r + STRIP, h : h + 1] - entries[:, :width]
                weight = gram[r : r + STRIP, :width] * jnp.exp2(jnp.minimum(power, 1.0))
                slot[r : r + STRIP, :width] = weight.astype(BF16)
        head = g * 32 + 2 * p
        skip = jnp.where(lane[0:1] < MHDIM, skip_ref[head], skip_ref[head + 1])
        for r, width in ((0, half), (half, ROWS)):
            first, second = (
                jnp.dot(
                    held[2 * (p % 2) + i, r : r + half, :width],
                    x_ref[:width, at],
                    preferred_element_type=F32,
                )
                for i in range(2)
            )
            rows = slice(r, r + half)
            y = jnp.where(lane < MHDIM, first, second) + skip * x_ref[rows, at].astype(F32)
            y_ref[rows, at] = y.astype(BF16)


def inside_call(group, x, b, c, row, col, skip):
    vmem = pl.BlockSpec(memory_space=pltpu.VMEM)
    smem = pl.BlockSpec(memory_space=pltpu.SMEM)
    return pl.pallas_call(
        inside_kernel,
        out_shape=jax.ShapeDtypeStruct((ROWS, GROUP_CHANNELS), BF16),
        in_specs=[smem, vmem, vmem, vmem, vmem, vmem, smem],
        out_specs=vmem,
        scratch_shapes=[pltpu.VMEM((ROWS, ROWS), F32), pltpu.VMEM((4, ROWS, ROWS), BF16)],
        compiler_params=params(),
        cost_estimate=cost(5e9, 3 * MIB),
        name="inside",
    )(group, x, b, c, row, col, skip)


def edge_of(s):
    return s[STATE : STATE + 1, :].astype(F32) + s[STATE + 1 : STATE + 2, :].astype(F32)


def combine_kernel(core_ref, own_ref, other_ref, out_ref):
    own_first = core_ref[0] == 0
    place = lax.broadcasted_iota(jnp.int32, (EXTRA, 128), 0)
    for p in range(PAIRS):
        own_edge, other_edge = edge_of(own_ref[p]), edge_of(other_ref[p])
        keep_own = jnp.where(own_first, other_edge, 1.0)
        keep_other = jnp.where(own_first, 1.0, own_edge)
        for r in range(0, STATE, STRIP):
            rows = slice(r, r + STRIP)
            own, other = own_ref[p, rows].astype(F32), other_ref[p, rows].astype(F32)
            out_ref[p, rows, :] = (keep_own * own + keep_other * other).astype(BF16)
        hi, lo = split_hi_lo(own_edge * other_edge)
        out_ref[p, STATE:SROWS, :] = jnp.where(
            place == 0, hi.astype(F32), jnp.where(place == 1, lo.astype(F32), 0.0)
        ).astype(BF16)


def combine_call(core, own, other):
    vmem = pl.BlockSpec(memory_space=pltpu.VMEM)
    return pl.pallas_call(
        combine_kernel,
        out_shape=jax.ShapeDtypeStruct((PAIRS, SROWS, 128), BF16),
        in_specs=[pl.BlockSpec(memory_space=pltpu.SMEM), vmem, vmem],
        out_specs=vmem,
        compiler_params=params(),
        cost_estimate=cost(2e9, 3 * MIB),
        name="combine",
    )(core, own, other)


def prefix_kernel(s_ref, out_ref):
    carried = jnp.zeros((STATE, 128), F32)
    for k in range(CHIPS):
        out_ref[k] = carried.astype(BF16)
        if k < CHIPS - 1:
            s = s_ref[k].astype(F32)
            carried = edge_of(s_ref[k]) * carried + s[:STATE]


def prefix_call(s):
    return pl.pallas_call(
        prefix_kernel,
        out_shape=jax.ShapeDtypeStruct((CHIPS, STATE, 128), BF16),
        in_specs=[pl.BlockSpec(memory_space=pltpu.VMEM)],
        out_specs=pl.BlockSpec(memory_space=pltpu.VMEM),
        compiler_params=params(),
        cost_estimate=cost(2e9, 2 * MIB),
        name="prefix",
    )(s)


def output_kernel(g_ref, s_ref, f_ref, c_ref, col_ref, y_ref, gate_ref, gain_ref, _, out_ref, held, state):
    group, core = g_ref[0], g_ref[1]

    @pl.when(pl.program_id(0) == 0)
    def _():
        for p in range(PAIRS):
            at = slice(p * LANES, (p + 1) * LANES)
            keep = jnp.where(core == 0, 1.0, edge_of(f_ref[p]))
            add = jnp.where(core == 0, 0.0, 1.0)
            for r in range(0, STATE, STRIP):
                rows = slice(r, r + STRIP)
                entering = keep * s_ref[p, rows].astype(F32) + add * f_ref[p, rows].astype(F32)
                state[rows, at] = entering.astype(BF16)

    rows = c_ref.shape[0]
    c = c_ref[...]
    grown = jnp.exp2(col_ref[:, 0:64])
    squares = jnp.zeros((rows, LANES), F32)
    for p in range(PAIRS):
        at = slice(p * LANES, (p + 1) * LANES)
        carried = jnp.dot(c, state[:, at], preferred_element_type=F32)
        factor = spread(grown, group * 32 + 2 * p, LANES)
        y = y_ref[:, at].astype(F32) + factor * carried
        gated = y * silu(gate_ref[:, at].astype(F32))
        squares = squares + gated * gated
        held[:, at] = gated
    mean = jnp.sum(squares, axis=1, keepdims=True) * (1.0 / GROUP_CHANNELS)
    scale = lax.rsqrt(mean + EPSILON)
    for p in range(PAIRS):
        at = slice(p * LANES, (p + 1) * LANES)
        out_ref[:, at] = (held[:, at] * scale * gain_ref[:, at].astype(F32)).astype(BF16)


def output_call(place, state, first, c, col, y, gate, gain, old):
    rows = 128
    whole = lambda n: pl.BlockSpec((PAIRS, n, 128), lambda i, g: (0, 0, 0))
    wide = pl.BlockSpec((rows, GROUP_CHANNELS), lambda i, g: (i, g[0]))
    in_specs = [
        whole(STATE),
        whole(SROWS),
        pl.BlockSpec((rows, STATE), lambda i, g: (i, 0)),
        pl.BlockSpec((rows, 128), lambda i, g: (i, 0)),
        pl.BlockSpec((rows, GROUP_CHANNELS), lambda i, g: (i, 0)),
        wide,
        pl.BlockSpec((1, GROUP_CHANNELS), lambda i, g: (0, g[0])),
    ]
    args = [place, state, first, c, col, y, gate, gain]
    if old is None:
        body = lambda *r: output_kernel(*r[:8], None, *r[8:])
        aliases = {}
    else:
        body = output_kernel
        in_specs.append(pl.BlockSpec(memory_space=pl.ANY))
        args.append(old)
        aliases = {8: 0}
    return pl.pallas_call(
        body,
        out_shape=jax.ShapeDtypeStruct((ROWS, 2 * GROUP_CHANNELS), BF16),
        grid_spec=pltpu.PrefetchScalarGridSpec(
            num_scalar_prefetch=1,
            grid=(ROWS // rows,),
            in_specs=in_specs,
            out_specs=wide,
            scratch_shapes=[
                pltpu.VMEM((rows, GROUP_CHANNELS), F32),
                pltpu.VMEM((STATE, GROUP_CHANNELS), BF16),
            ],
        ),
        input_output_aliases=aliases,
        compiler_params=params(),
        cost_estimate=cost(4e9, 5 * MIB),
        name="mixer_out",
    )(*args)


UNIT = 1024
SLOTS = 4
QPER = 8
SHARE_LANES = SLOTS * HDIM
SCALE = LOG2E * HDIM ** (-0.5)
OFFSETS = (0, -1, 1, 2)
HALF = QPER * HDIM


def given(chip):
    return jnp.where(chip >= 14, 2, jnp.where(chip >= 10, 1, 0))


def attention_kernel(kinds, pieces, scal, *refs):
    queries = refs[: len(kinds)]
    kv_refs = refs[len(kinds) : len(kinds) + pieces]
    outs = refs[len(kinds) + pieces : -5]
    kv, qs, acc, result, sem = refs[-5:]
    core, chip = scal[0], scal[1]
    y, x = chip // NX, lax.rem(chip, NX)
    rows_of_chip = NCORE * ROWS
    copies = []
    for n in range(CHIPS):
        two, one = OFFSETS[n // NX], OFFSETS[n % NX]
        dy, dx = jnp.where(core == 0, two, one), jnp.where(core == 0, one, two)
        unit = lax.rem(y + dy + NY, NY) * NX + lax.rem(x + dx + NX, NX)
        source = kv_refs[n // 2].at[pl.ds((n % 2) * rows_of_chip, rows_of_chip)]
        to = pl.ds(pl.multiple_of(unit * rows_of_chip, rows_of_chip), rows_of_chip)
        copies.append(pltpu.make_async_copy(source, kv.at[to], sem.at[n]))
        copies[-1].start()
    for n, ref in enumerate(queries):
        for h in range(QPER):
            at = pl.ds(h * HDIM, HDIM)
            if kinds[n] == "own":
                at = pl.ds(pl.multiple_of(core * HALF + h * HDIM, HDIM), HDIM)
            hi, lo = split_hi_lo(ref[:, at].astype(F32) * SCALE)
            qs[n * QPER + h, :, 0:HDIM] = hi
            qs[n * QPER + h, :, HDIM:] = lo
    for copy in copies:
        copy.wait()
    give, take = given(chip), given(CHIPS - 1 - chip)
    shares = 2 * len(kinds)

    def share(j, carry):
        kind = j // 2
        second = lax.rem(j, 2)
        far = kind == 2
        its_chip = jnp.where(far, CHIPS - 1 - chip, chip)
        its_core = jnp.where(kind == 0, core, 1 - core)
        used = jnp.where(
            kind == 0, True, jnp.where(far, take >= 2 - second, give <= 1 - second)
        )
        limit = its_chip // 2
        first_row = lax.rem(its_chip, 2) * rows_of_chip + its_core * ROWS

        def scores_of(slot, keys):
            return lax.dot_general(
                qs[j * SLOTS + slot], keys, (((1,), (1,)), ((), ())), preferred_element_type=F32
            )

        def keys_values_of(u):
            rows = pl.ds(pl.multiple_of(u * UNIT, UNIT), UNIT)
            keys, values = kv[rows, 0:HDIM], kv[rows, HDIM:]
            keys = jnp.concatenate([keys, keys], 1)
            return keys, jnp.concatenate([values, jnp.ones((UNIT, HDIM), BF16)], 1)

        def visible_in(shift):
            row = lax.broadcasted_iota(jnp.int32, (ROWS, UNIT), 0) + first_row
            col = lax.broadcasted_iota(jnp.int32, (ROWS, UNIT), 1)
            return col + shift <= row

        def absorb(u, masked):
            keys, values = keys_values_of(u)
            scores = [scores_of(h, keys) for h in range(SLOTS)]
            for h in range(SLOTS):
                p = jnp.exp2(scores[h])
                if masked:
                    p = jnp.where(visible_in(0), p, 0.0)
                got = jnp.dot(p.astype(BF16), values, preferred_element_type=F32)
                acc[h] = got if masked else acc[h] + got

        @pl.when(used)
        def _():
            absorb(limit, True)

            def one(u, carry):
                absorb(u, False)
                return carry

            lax.fori_loop(0, limit, one, 0)
            least = jnp.full((ROWS, HDIM), 1.0, F32)
            most = jnp.full((ROWS, HDIM), 1.0, F32)
            for h in range(SLOTS):
                total = acc[h, :, HDIM:]
                least = jnp.minimum(least, total)
                most = jnp.maximum(most, total)
                result[j, :, h * HDIM : (h + 1) * HDIM] = (acc[h, :, :HDIM] / total).astype(BF16)
            safe = (jnp.min(least) > 2.0**-80) & (jnp.max(most) < 2.0**110)

            @pl.when(jnp.logical_not(safe))
            def _():
                def head(h, carry):
                    def unit_step(u, state):
                        top, total, summed = state
                        keys, values = keys_values_of(u)
                        shown = visible_in((u - limit) * UNIT)
                        scores = jnp.where(shown, scores_of(h, keys), -1e30)
                        new_top = jnp.maximum(top, jnp.max(scores, axis=1, keepdims=True))
                        shrink = jnp.exp2(top - new_top)
                        p = jnp.where(shown, jnp.exp2(scores - new_top), 0.0)
                        total = total * shrink + jnp.sum(p, axis=1, keepdims=True)
                        summed = summed * shrink + jnp.dot(
                            p.astype(BF16), values[:, :HDIM], preferred_element_type=F32
                        )
                        return new_top, total, summed

                    zero = jnp.zeros((ROWS, 1), F32)
                    state = (zero - 1e30, zero, jnp.zeros((ROWS, HDIM), F32))
                    _, total, summed = lax.fori_loop(0, limit + 1, unit_step, state)
                    at = pl.ds(pl.multiple_of(h * HDIM, HDIM), HDIM)
                    result[j, :, at] = (summed / total).astype(BF16)
                    return carry

                lax.fori_loop(0, SLOTS, head, 0)

        return carry

    lax.fori_loop(0, shares, share, 0)
    for j in range(shares):
        outs[j // 2][:, (j % 2) * SHARE_LANES : (j % 2 + 1) * SHARE_LANES] = result[j]


def attention_call(scal, kinds, queries, pieces):
    vmem = pl.BlockSpec(memory_space=pltpu.VMEM)
    slots = QPER * len(kinds)

    def body(*refs):
        attention_kernel(kinds, len(pieces), *refs)

    return pl.pallas_call(
        body,
        out_shape=tuple(jax.ShapeDtypeStruct((ROWS, HALF), BF16) for _ in kinds),
        in_specs=[pl.BlockSpec(memory_space=pltpu.SMEM)]
        + [vmem] * len(kinds)
        + [pl.BlockSpec(memory_space=pl.ANY)] * len(pieces),
        out_specs=tuple(vmem for _ in kinds),
        scratch_shapes=[
            pltpu.VMEM((CHIPS * NCORE * ROWS, 2 * HDIM), BF16),
            pltpu.VMEM((slots, ROWS, 2 * HDIM), BF16),
            pltpu.VMEM((SLOTS, ROWS, 2 * HDIM), F32),
            pltpu.VMEM((2 * len(kinds), ROWS, SHARE_LANES), BF16),
            pltpu.SemaphoreType.DMA((CHIPS,)),
        ],
        compiler_params=params(58),
        cost_estimate=cost(3e10, 8 * MIB),
        name="attention",
    )(scal, *queries, *pieces)


def join_kernel(first, second, third, fourth, front_ref, back_ref):
    rows = first.shape[0]
    front_ref[0:rows] = first[...]
    front_ref[rows:] = second[...]
    back_ref[0:rows] = third[...]
    back_ref[rows:] = fourth[...]


def join_call(*parts):
    vmem = pl.BlockSpec(memory_space=pltpu.VMEM)
    rows, width = parts[0].shape
    return pl.pallas_call(
        join_kernel,
        out_shape=(jax.ShapeDtypeStruct((2 * rows, width), BF16),) * 2,
        in_specs=[vmem] * 4,
        out_specs=(vmem, vmem),
        compiler_params=params(),
        cost_estimate=cost(1e9, 2 * MIB),
        name="join",
    )(*parts)


def permute(value, target):
    pairs = []
    for place in range(NY * NX * NCORE):
        y, x, c = place // (NX * NCORE), (place // NCORE) % NX, place % NCORE
        y, x, c = target(y, x, c)
        pairs.append((place, ((y % NY) * NX + x % NX) * NCORE + c))
    return lax.ppermute(value, "seq", pairs)


def swap(value):
    return permute(value, lambda y, x, c: (y, x, 1 - c))


def along(value, step, second):
    def target(y, x, c):
        return (y, x + step, c) if c == second else (y + step, x, c)

    return permute(value, target)


ALL_CHIPS = [[chip * NCORE + core for chip in range(CHIPS)] for core in range(NCORE)]


def exchange(value):
    return lax.all_to_all(value, "seq", 0, 0, axis_index_groups=ALL_CHIPS, tiled=True)


def mirror(value, to_low):
    seq = CHIPS * NCORE
    pairs = [(place, seq - 1 - place) for place in range(10 * NCORE, seq)]
    return lax.ppermute(value, "seq", pairs if to_low else [(low, high) for high, low in pairs])


def local(
    token_ids,
    token_tables,
    ssm_input,
    ssm_gate,
    ssm_bc,
    conv_input,
    conv_bc,
    skip_gain,
    norm_gain,
    queries,
    keys_values,
):
    place = lax.axis_index("seq")
    core = lax.rem(place, NCORE)
    chip = place // NCORE
    keep = core.reshape(1)

    kv = keys_values.reshape(ROWS, 4, HDIM)
    zero = jnp.concatenate([kv[:, 0], kv[:, 2]], 1)
    one = jnp.concatenate([kv[:, 1], kv[:, 3]], 1)
    mine = jnp.where(core == 0, zero, one)
    from_other = swap(jnp.where(core == 0, one, zero))

    bc = ssm_bc.reshape(ROWS, -1)
    edge = jnp.concatenate([ssm_input[ROWS - 16 :], bc[ROWS - 16 :]], 1)
    seq = NY * NX * NCORE
    front = lax.ppermute(edge, "seq", [(i, i + 1) for i in range(seq - 1)])

    scal = jnp.stack([core, chip]).astype(jnp.int32)
    together = lax.optimization_barrier

    query_other = lax.dynamic_slice_in_dim(queries, (1 - core) * HALF, HALF, 1)
    near = swap(query_other)
    far = mirror(query_other, True)
    row, col = table_call(token_ids, token_tables)
    from_other, row, col = together((from_other, row, col))
    unit = jnp.where(
        core == 0,
        jnp.concatenate([mine, from_other], 0),
        jnp.concatenate([from_other, mine], 0),
    )
    left, right, across = (along(unit, step, 0) for step in (1, -1, 2))
    taps_bc = conv_bc.reshape(CONV, -1)
    send = 1 - keep
    x_s, b_s, c_s, state_s = state_call(send, ssm_input, front, conv_input, bc, taps_bc, col)
    state_o = swap(state_s)
    left, right, across, x_s = together((left, right, across, x_s))
    line_a, line_b = join_call(unit, left, right, across)
    left_a, right_b = along(line_a, 1, 1), along(line_b, -1, 1)
    left_b, right_a = along(line_b, 1, 1), along(line_a, -1, 1)
    line_a, line_b, col_k = together((line_a, line_b, col))
    x_k, b_k, c_k, state_k = state_call(keep, ssm_input, front, conv_input, bc, taps_bc, col_k)
    joined = combine_call(keep, state_k, state_o)
    joined, x_s, x_k = together((joined, x_s, x_k))
    arrived = exchange(joined)
    left_a, right_b, left_b, right_a, near, far, x_s = together(
        (left_a, right_b, left_b, right_a, near, far, x_s)
    )
    across_a, across_b = along(left_a, 1, 1), along(right_b, -1, 1)
    y_s = inside_call(send, x_s, b_s, c_s, row, col, skip_gain)
    y_k = inside_call(keep, x_k, b_k, c_k, row, col, skip_gain)
    pieces = [line_a, line_b, left_a, left_b, right_a, right_b, across_a, across_b]
    arrived, y_k, y_s, state_k = together((arrived, y_k, y_s, state_k))
    first_s = swap(state_k)
    before = prefix_call(arrived)
    entering_k = exchange(before)
    scal, before = together((scal, before))
    own, near_out, far_out = attention_call(
        scal, ("own", "near", "far"), [queries, near, far], pieces
    )
    y_k, y_s, far_out, near_out, entering_k = together((y_k, y_s, far_out, near_out, entering_k))
    entering_s = swap(entering_k)
    back, near_back = mirror(far_out, False), swap(near_out)

    gain = norm_gain.reshape(1, -1)
    place_k = jnp.stack([core, core]).astype(jnp.int32)
    place_s = jnp.stack([1 - core, core]).astype(jnp.int32)
    mixed = output_call(place_k, entering_k, state_o, c_k, col, y_k, ssm_gate, gain, None)
    mixed = output_call(place_s, entering_s, first_s, c_s, col, y_s, ssm_gate, gain, mixed)
    give = given(chip)
    mixed, back, near_back = together((mixed, back, near_back))
    other = jnp.concatenate(
        [
            jnp.where(give >= 2, back[:, :SHARE_LANES], near_back[:, :SHARE_LANES]),
            jnp.where(give >= 1, back[:, SHARE_LANES:], near_back[:, SHARE_LANES:]),
        ],
        1,
    )
    attn = jnp.where(
        core == 0, jnp.concatenate([own, other], 1), jnp.concatenate([other, own], 1)
    )
    return mixed, attn


def solution(mesh):
    in_specs = (
        P(("dp", "seq")),
        P(None, "head", None),
        P(("dp", "seq"), "head"),
        P(("dp", "seq"), "head"),
        P(("dp", "seq"), None, "head"),
        P(None, "head"),
        P(None, None, "head"),
        P("head"),
        P("head"),
        P(("dp", "seq"), "head"),
        P(("dp", "seq"), None, "head"),
    )
    out_specs = (P(("dp", "seq"), "head"), P(("dp", "seq"), "head"))
    return jax.shard_map(local, mesh=mesh, in_specs=in_specs, out_specs=out_specs, check_vma=False)
```

```python
import math

import jax
import jax.numpy as jnp
from jax import lax
from jax.experimental import pallas as pl
from jax.experimental.pallas import tpu as pltpu
from jax.sharding import PartitionSpec as P

MHDIM = 64
STATE = 256
CONV = 4
HDIM = 128
EPSILON = 1e-05
LOG2E = math.log2(math.e)
F32 = jnp.float32
BF16 = jnp.bfloat16

NY, NX, NCORE = 4, 4, 2
CHIPS = NY * NX
ROWS = 256
GROUP_CHANNELS = 2048
PAIRS = 16
EXTRA = 16
SROWS = STATE + EXTRA
MIB = 1 << 20


def params(mib=24):
    return pltpu.CompilerParams(vmem_limit_bytes=mib * MIB)


def cost(flops, nbytes, trans=0):
    return pl.CostEstimate(flops=int(flops), bytes_accessed=int(nbytes), transcendentals=int(trans))


def silu(v):
    half = 0.5 * v
    return half + half * jnp.tanh(half)


def split_hi_lo(v):
    hi = v.astype(BF16)
    lo = (v - hi.astype(F32)).astype(BF16)
    return hi, lo


def table_kernel(ids_ref, tab_ref, row_ref, col_ref, acc):
    step = pl.program_id(0)
    width = tab_ref.shape[2]

    @pl.when(step == 0)
    def _():
        acc[...] = jnp.zeros_like(acc)

    part = 1024
    for i in range(width // part):
        places = lax.broadcasted_iota(jnp.int32, (part, ROWS), 0) + (step * width + i * part)
        hot = jnp.where(places == ids_ref[...], 1.0, 0.0).astype(BF16)
        table = tab_ref[:, :, i * part : (i + 1) * part].reshape(128, part)
        acc[...] += jnp.dot(table, hot, preferred_element_type=F32)

    @pl.when(step == pl.num_programs(0) - 1)
    def _():
        u = lax.broadcasted_iota(jnp.int32, (ROWS, ROWS), 0)
        t = lax.broadcasted_iota(jnp.int32, (ROWS, ROWS), 1)
        tri = jnp.where(u <= t, 1.0, 0.0).astype(BF16)
        rate, raw = acc[0:64, :], acc[64:128, :]
        cum = jnp.dot(rate.astype(BF16), tri, preferred_element_type=F32) * (-LOG2E)
        size = jnp.maximum(raw, 0.0) + jnp.log1p(jnp.exp(-jnp.abs(raw)))
        both = jnp.concatenate([cum, cum - jnp.log(size) * LOG2E], 0)
        row_ref[...] = both
        col_ref[...] = both.T


def table_call(token_ids, token_tables):
    width = 4096
    return pl.pallas_call(
        table_kernel,
        out_shape=(
            jax.ShapeDtypeStruct((128, ROWS), F32),
            jax.ShapeDtypeStruct((ROWS, 128), F32),
        ),
        grid=(token_tables.shape[2] // width,),
        in_specs=[
            pl.BlockSpec((1, ROWS), lambda i: (0, 0)),
            pl.BlockSpec((2, 64, width), lambda i: (0, 0, i)),
        ],
        out_specs=[
            pl.BlockSpec((128, ROWS), lambda i: (0, 0)),
            pl.BlockSpec((ROWS, 128), lambda i: (0, 0)),
        ],
        scratch_shapes=[pltpu.VMEM((128, ROWS), F32)],
        compiler_params=params(),
        cost_estimate=cost(4e9, 2 * MIB),
        name="tables",
    )(token_ids.reshape(1, ROWS), token_tables)


def spread(values, first_head, width):
    hi, lo = split_hi_lo(values)
    r = lax.broadcasted_iota(jnp.int32, (64, width), 0)
    ch = lax.broadcasted_iota(jnp.int32, (64, width), 1)
    hot = jnp.where(r == first_head + ch // MHDIM, 1.0, 0.0).astype(BF16)
    return jnp.dot(
        jnp.concatenate([hi, lo], 1),
        jnp.concatenate([hot, hot], 0),
        preferred_element_type=F32,
    )


LANES = 128
STRIP = 64


def conv_strips(values_ref, front_ref, taps_ref, at, buffer, out_ref):
    buffer[0:16, :] = front_ref[:, at].astype(F32)
    for r in range(0, ROWS, STRIP):
        buffer[16 + r : 16 + r + STRIP, :] = values_ref[r : r + STRIP, at].astype(F32)
    taps = taps_ref[:, at].astype(F32)
    for r in range(0, ROWS, STRIP):
        total = taps[CONV - 1 : CONV] * buffer[16 + r : 16 + r + STRIP, :]
        for k in range(CONV - 1):
            total = total + taps[k : k + 1] * buffer[13 + k + r : 13 + k + r + STRIP, :]
        out_ref[r : r + STRIP, at] = silu(total).astype(BF16)


def state_kernel(group_ref, *refs):
    x_ref, xf_ref, xt_ref, b_ref, bf_ref, bt_ref, c_ref, cf_ref, ct_ref, col_ref = refs[:10]
    xc_ref, bc_ref, cc_ref, s_ref, buffer, scaled = refs[10:]
    group = group_ref[0]
    for i in range(STATE // LANES):
        at = slice(i * LANES, (i + 1) * LANES)
        conv_strips(b_ref, bf_ref, bt_ref, at, buffer.at[i], bc_ref)
        conv_strips(c_ref, cf_ref, ct_ref, at, buffer.at[2 + i], cc_ref)
    btrans = bc_ref[...].astype(F32).T.astype(BF16)
    last = col_ref[ROWS - 1 : ROWS, 0:64]
    tail = jnp.exp2(last - col_ref[:, 64:128])
    weights = jnp.concatenate([tail, jnp.broadcast_to(jnp.exp2(last), (EXTRA, 64))], 0)
    place = lax.broadcasted_iota(jnp.int32, (EXTRA, LANES), 0)
    for p in range(PAIRS):
        at = slice(p * LANES, (p + 1) * LANES)
        conv_strips(x_ref, xf_ref, xt_ref, at, buffer.at[p % 4], xc_ref)
        wide = spread(weights, group * 32 + 2 * p, LANES)
        for r in range(0, ROWS, STRIP):
            rows = slice(r, r + STRIP)
            scaled[p % 4, rows, :] = (xc_ref[rows, at].astype(F32) * wide[rows]).astype(BF16)
        state = jnp.dot(btrans, scaled[p % 4], preferred_element_type=F32)
        s_ref[p, 0:STATE, :] = state.astype(BF16)
        hi, lo = split_hi_lo(wide[ROWS:])
        edge = jnp.where(place == 0, hi.astype(F32), jnp.where(place == 1, lo.astype(F32), 0.0))
        s_ref[p, STATE:SROWS, :] = edge.astype(BF16)


def state_call(group, ssm_input, front, conv_input, bc, conv_bc, col):
    wide = lambda rows: pl.BlockSpec((rows, GROUP_CHANNELS), lambda j, g: (0, g[0]))
    narrow = lambda rows, base: pl.BlockSpec((rows, STATE), lambda j, g: (0, base + g[0]))
    whole = lambda shape: pl.BlockSpec(shape, lambda j, g: (0,) * len(shape))
    shapes = ((ROWS, GROUP_CHANNELS), (ROWS, STATE), (ROWS, STATE), (PAIRS, SROWS, 128))
    return pl.pallas_call(
        state_kernel,
        out_shape=tuple(jax.ShapeDtypeStruct(shape, BF16) for shape in shapes),
        grid_spec=pltpu.PrefetchScalarGridSpec(
            num_scalar_prefetch=1,
            grid=(1,),
            in_specs=[
                wide(ROWS),
                wide(16),
                wide(CONV),
                narrow(ROWS, 0),
                narrow(16, 16),
                narrow(CONV, 0),
                narrow(ROWS, 2),
                narrow(16, 18),
                narrow(CONV, 2),
                whole((ROWS, 128)),
            ],
            out_specs=[whole(shape) for shape in shapes],
            scratch_shapes=[
                pltpu.VMEM((4, 16 + ROWS, LANES), F32),
                pltpu.VMEM((4, ROWS, LANES), BF16),
            ],
        ),
        compiler_params=params(),
        cost_estimate=cost(4e9, 3 * MIB),
        name="conv_state",
    )(group, ssm_input, front, conv_input, bc, front, conv_bc, bc, front, conv_bc, col)


def inside_kernel(g_ref, x_ref, b_ref, c_ref, row_ref, col_ref, skip_ref, y_ref, gram, held):
    g = g_ref[0]
    half = ROWS // 2
    product = lax.dot_general(
        c_ref[...], b_ref[...], (((1,), (1,)), ((), ())), preferred_element_type=F32
    )
    t = lax.broadcasted_iota(jnp.int32, (ROWS, ROWS), 0)
    s = lax.broadcasted_iota(jnp.int32, (ROWS, ROWS), 1)
    gram[...] = jnp.where(s <= t, product, 0.0)
    columns = pltpu.roll(col_ref[...], lax.rem(128 - g * 32, 128), 1)
    lane = lax.broadcasted_iota(jnp.int32, (half, LANES), 1)
    for p in range(PAIRS):
        at = slice(p * LANES, (p + 1) * LANES)
        for i in range(2):
            h = 2 * p + i
            entries = row_ref[pl.ds(64 + g * 32 + h, 1), :]
            slot = held.at[2 * (p % 2) + i]
            for r in range(0, ROWS, STRIP):
                width = half if r < half else ROWS
                power = columns[r : r + STRIP, h : h + 1] - entries[:, :width]
                weight = gram[r : r + STRIP, :width] * jnp.exp2(jnp.minimum(power, 1.0))
                slot[r : r + STRIP, :width] = weight.astype(BF16)
        head = g * 32 + 2 * p
        skip = jnp.where(lane[0:1] < MHDIM, skip_ref[head], skip_ref[head + 1])
        for r, width in ((0, half), (half, ROWS)):
            first, second = (
                jnp.dot(
                    held[2 * (p % 2) + i, r : r + half, :width],
                    x_ref[:width, at],
                    preferred_element_type=F32,
                )
                for i in range(2)
            )
            rows = slice(r, r + half)
            y = jnp.where(lane < MHDIM, first, second) + skip * x_ref[rows, at].astype(F32)
            y_ref[rows, at] = y.astype(BF16)


def inside_call(group, x, b, c, row, col, skip):
    vmem = pl.BlockSpec(memory_space=pltpu.VMEM)
    smem = pl.BlockSpec(memory_space=pltpu.SMEM)
    return pl.pallas_call(
        inside_kernel,
        out_shape=jax.ShapeDtypeStruct((ROWS, GROUP_CHANNELS), BF16),
        in_specs=[smem, vmem, vmem, vmem, vmem, vmem, smem],
        out_specs=vmem,
        scratch_shapes=[pltpu.VMEM((ROWS, ROWS), F32), pltpu.VMEM((4, ROWS, ROWS), BF16)],
        compiler_params=params(),
        cost_estimate=cost(5e9, 3 * MIB),
        name="inside",
    )(group, x, b, c, row, col, skip)


def edge_of(s):
    return s[STATE : STATE + 1, :].astype(F32) + s[STATE + 1 : STATE + 2, :].astype(F32)


def combine_kernel(core_ref, own_ref, other_ref, out_ref):
    own_first = core_ref[0] == 0
    place = lax.broadcasted_iota(jnp.int32, (EXTRA, 128), 0)
    for p in range(PAIRS):
        own_edge, other_edge = edge_of(own_ref[p]), edge_of(other_ref[p])
        keep_own = jnp.where(own_first, other_edge, 1.0)
        keep_other = jnp.where(own_first, 1.0, own_edge)
        for r in range(0, STATE, STRIP):
            rows = slice(r, r + STRIP)
            own, other = own_ref[p, rows].astype(F32), other_ref[p, rows].astype(F32)
            out_ref[p, rows, :] = (keep_own * own + keep_other * other).astype(BF16)
        hi, lo = split_hi_lo(own_edge * other_edge)
        out_ref[p, STATE:SROWS, :] = jnp.where(
            place == 0, hi.astype(F32), jnp.where(place == 1, lo.astype(F32), 0.0)
        ).astype(BF16)


def combine_call(core, own, other):
    vmem = pl.BlockSpec(memory_space=pltpu.VMEM)
    return pl.pallas_call(
        combine_kernel,
        out_shape=jax.ShapeDtypeStruct((PAIRS, SROWS, 128), BF16),
        in_specs=[pl.BlockSpec(memory_space=pltpu.SMEM), vmem, vmem],
        out_specs=vmem,
        compiler_params=params(),
        cost_estimate=cost(2e9, 3 * MIB),
        name="combine",
    )(core, own, other)


def prefix_kernel(s_ref, out_ref):
    carried = jnp.zeros((STATE, 128), F32)
    for k in range(CHIPS):
        out_ref[k] = carried.astype(BF16)
        if k < CHIPS - 1:
            s = s_ref[k].astype(F32)
            carried = edge_of(s_ref[k]) * carried + s[:STATE]


def prefix_call(s):
    return pl.pallas_call(
        prefix_kernel,
        out_shape=jax.ShapeDtypeStruct((CHIPS, STATE, 128), BF16),
        in_specs=[pl.BlockSpec(memory_space=pltpu.VMEM)],
        out_specs=pl.BlockSpec(memory_space=pltpu.VMEM),
        compiler_params=params(),
        cost_estimate=cost(2e9, 2 * MIB),
        name="prefix",
    )(s)


def output_kernel(g_ref, s_ref, f_ref, c_ref, col_ref, y_ref, gate_ref, gain_ref, _, out_ref, held, state):
    group, core = g_ref[0], g_ref[1]

    @pl.when(pl.program_id(0) == 0)
    def _():
        for p in range(PAIRS):
            at = slice(p * LANES, (p + 1) * LANES)
            keep = jnp.where(core == 0, 1.0, edge_of(f_ref[p]))
            add = jnp.where(core == 0, 0.0, 1.0)
            for r in range(0, STATE, STRIP):
                rows = slice(r, r + STRIP)
                entering = keep * s_ref[p, rows].astype(F32) + add * f_ref[p, rows].astype(F32)
                state[rows, at] = entering.astype(BF16)

    rows = c_ref.shape[0]
    c = c_ref[...]
    grown = jnp.exp2(col_ref[:, 0:64])
    squares = jnp.zeros((rows, LANES), F32)
    for p in range(PAIRS):
        at = slice(p * LANES, (p + 1) * LANES)
        carried = jnp.dot(c, state[:, at], preferred_element_type=F32)
        factor = spread(grown, group * 32 + 2 * p, LANES)
        y = y_ref[:, at].astype(F32) + factor * carried
        gated = y * silu(gate_ref[:, at].astype(F32))
        squares = squares + gated * gated
        held[:, at] = gated
    mean = jnp.sum(squares, axis=1, keepdims=True) * (1.0 / GROUP_CHANNELS)
    scale = lax.rsqrt(mean + EPSILON)
    for p in range(PAIRS):
        at = slice(p * LANES, (p + 1) * LANES)
        out_ref[:, at] = (held[:, at] * scale * gain_ref[:, at].astype(F32)).astype(BF16)


def output_call(place, state, first, c, col, y, gate, gain, old):
    rows = 128
    whole = lambda n: pl.BlockSpec((PAIRS, n, 128), lambda i, g: (0, 0, 0))
    wide = pl.BlockSpec((rows, GROUP_CHANNELS), lambda i, g: (i, g[0]))
    in_specs = [
        whole(STATE),
        whole(SROWS),
        pl.BlockSpec((rows, STATE), lambda i, g: (i, 0)),
        pl.BlockSpec((rows, 128), lambda i, g: (i, 0)),
        pl.BlockSpec((rows, GROUP_CHANNELS), lambda i, g: (i, 0)),
        wide,
        pl.BlockSpec((1, GROUP_CHANNELS), lambda i, g: (0, g[0])),
    ]
    args = [place, state, first, c, col, y, gate, gain]
    if old is None:
        body = lambda *r: output_kernel(*r[:8], None, *r[8:])
        aliases = {}
    else:
        body = output_kernel
        in_specs.append(pl.BlockSpec(memory_space=pl.ANY))
        args.append(old)
        aliases = {8: 0}
    return pl.pallas_call(
        body,
        out_shape=jax.ShapeDtypeStruct((ROWS, 2 * GROUP_CHANNELS), BF16),
        grid_spec=pltpu.PrefetchScalarGridSpec(
            num_scalar_prefetch=1,
            grid=(ROWS // rows,),
            in_specs=in_specs,
            out_specs=wide,
            scratch_shapes=[
                pltpu.VMEM((rows, GROUP_CHANNELS), F32),
                pltpu.VMEM((STATE, GROUP_CHANNELS), BF16),
            ],
        ),
        input_output_aliases=aliases,
        compiler_params=params(),
        cost_estimate=cost(4e9, 5 * MIB),
        name="mixer_out",
    )(*args)


UNIT = 1024
SLOTS = 4
QPER = 8
SHARE_LANES = SLOTS * HDIM
SCALE = LOG2E * HDIM ** (-0.5)
OFFSETS = (0, -1, 1, 2)
HALF = QPER * HDIM


def given(chip):
    return jnp.where(chip >= 14, 2, jnp.where(chip >= 10, 1, 0))


def attention_kernel(kinds, pieces, scal, *refs):
    queries = refs[: len(kinds)]
    kv_refs = refs[len(kinds) : len(kinds) + pieces]
    outs = refs[len(kinds) + pieces : -5]
    kv, qs, acc, result, sem = refs[-5:]
    core, chip = scal[0], scal[1]
    y, x = chip // NX, lax.rem(chip, NX)
    rows_of_chip = NCORE * ROWS
    copies = []
    for n in range(CHIPS):
        two, one = OFFSETS[n // NX], OFFSETS[n % NX]
        dy, dx = jnp.where(core == 0, two, one), jnp.where(core == 0, one, two)
        unit = lax.rem(y + dy + NY, NY) * NX + lax.rem(x + dx + NX, NX)
        source = kv_refs[n // 2].at[pl.ds((n % 2) * rows_of_chip, rows_of_chip)]
        to = pl.ds(pl.multiple_of(unit * rows_of_chip, rows_of_chip), rows_of_chip)
        copies.append(pltpu.make_async_copy(source, kv.at[to], sem.at[n]))
        copies[-1].start()
    for n, ref in enumerate(queries):
        for h in range(QPER):
            at = pl.ds(h * HDIM, HDIM)
            if kinds[n] == "own":
                at = pl.ds(pl.multiple_of(core * HALF + h * HDIM, HDIM), HDIM)
            hi, lo = split_hi_lo(ref[:, at].astype(F32) * SCALE)
            qs[n * QPER + h, :, 0:HDIM] = hi
            qs[n * QPER + h, :, HDIM:] = lo
    for copy in copies:
        copy.wait()
    give, take = given(chip), given(CHIPS - 1 - chip)
    shares = 2 * len(kinds)

    def share(j, carry):
        kind = j // 2
        second = lax.rem(j, 2)
        far = kind == 2
        its_chip = jnp.where(far, CHIPS - 1 - chip, chip)
        its_core = jnp.where(kind == 0, core, 1 - core)
        used = jnp.where(
            kind == 0, True, jnp.where(far, take >= 2 - second, give <= 1 - second)
        )
        limit = its_chip // 2
        first_row = lax.rem(its_chip, 2) * rows_of_chip + its_core * ROWS

        def scores_of(slot, keys):
            return lax.dot_general(
                qs[j * SLOTS + slot], keys, (((1,), (1,)), ((), ())), preferred_element_type=F32
            )

        def keys_values_of(u):
            rows = pl.ds(pl.multiple_of(u * UNIT, UNIT), UNIT)
            keys, values = kv[rows, 0:HDIM], kv[rows, HDIM:]
            keys = jnp.concatenate([keys, keys], 1)
            return keys, jnp.concatenate([values, jnp.ones((UNIT, HDIM), BF16)], 1)

        def visible_in(shift):
            row = lax.broadcasted_iota(jnp.int32, (ROWS, UNIT), 0) + first_row
            col = lax.broadcasted_iota(jnp.int32, (ROWS, UNIT), 1)
            return col + shift <= row

        def absorb(u, masked):
            keys, values = keys_values_of(u)
            scores = [scores_of(h, keys) for h in range(SLOTS)]
            for h in range(SLOTS):
                p = jnp.exp2(scores[h])
                if masked:
                    p = jnp.where(visible_in(0), p, 0.0)
                got = jnp.dot(p.astype(BF16), values, preferred_element_type=F32)
                acc[h] = got if masked else acc[h] + got

        @pl.when(used)
        def _():
            absorb(limit, True)

            def one(u, carry):
                absorb(u, False)
                return carry

            lax.fori_loop(0, limit, one, 0)
            least = jnp.full((ROWS, HDIM), 1.0, F32)
            most = jnp.full((ROWS, HDIM), 1.0, F32)
            for h in range(SLOTS):
                total = acc[h, :, HDIM:]
                least = jnp.minimum(least, total)
                most = jnp.maximum(most, total)
                result[j, :, h * HDIM : (h + 1) * HDIM] = (acc[h, :, :HDIM] / total).astype(BF16)
            safe = (jnp.min(least) > 2.0**-80) & (jnp.max(most) < 2.0**110)

            @pl.when(jnp.logical_not(safe))
            def _():
                def head(h, carry):
                    def unit_step(u, state):
                        top, total, summed = state
                        keys, values = keys_values_of(u)
                        shown = visible_in((u - limit) * UNIT)
                        scores = jnp.where(shown, scores_of(h, keys), -1e30)
                        new_top = jnp.maximum(top, jnp.max(scores, axis=1, keepdims=True))
                        shrink = jnp.exp2(top - new_top)
                        p = jnp.where(shown, jnp.exp2(scores - new_top), 0.0)
                        total = total * shrink + jnp.sum(p, axis=1, keepdims=True)
                        summed = summed * shrink + jnp.dot(
                            p.astype(BF16), values[:, :HDIM], preferred_element_type=F32
                        )
                        return new_top, total, summed

                    zero = jnp.zeros((ROWS, 1), F32)
                    state = (zero - 1e30, zero, jnp.zeros((ROWS, HDIM), F32))
                    _, total, summed = lax.fori_loop(0, limit + 1, unit_step, state)
                    at = pl.ds(pl.multiple_of(h * HDIM, HDIM), HDIM)
                    result[j, :, at] = (summed / total).astype(BF16)
                    return carry

                lax.fori_loop(0, SLOTS, head, 0)

        return carry

    lax.fori_loop(0, shares, share, 0)
    for j in range(shares):
        outs[j // 2][:, (j % 2) * SHARE_LANES : (j % 2 + 1) * SHARE_LANES] = result[j]


def attention_call(scal, kinds, queries, pieces):
    vmem = pl.BlockSpec(memory_space=pltpu.VMEM)
    slots = QPER * len(kinds)

    def body(*refs):
        attention_kernel(kinds, len(pieces), *refs)

    return pl.pallas_call(
        body,
        out_shape=tuple(jax.ShapeDtypeStruct((ROWS, HALF), BF16) for _ in kinds),
        in_specs=[pl.BlockSpec(memory_space=pltpu.SMEM)]
        + [vmem] * len(kinds)
        + [pl.BlockSpec(memory_space=pl.ANY)] * len(pieces),
        out_specs=tuple(vmem for _ in kinds),
        scratch_shapes=[
            pltpu.VMEM((CHIPS * NCORE * ROWS, 2 * HDIM), BF16),
            pltpu.VMEM((slots, ROWS, 2 * HDIM), BF16),
            pltpu.VMEM((SLOTS, ROWS, 2 * HDIM), F32),
            pltpu.VMEM((2 * len(kinds), ROWS, SHARE_LANES), BF16),
            pltpu.SemaphoreType.DMA((CHIPS,)),
        ],
        compiler_params=params(58),
        cost_estimate=cost(3e10, 8 * MIB),
        name="attention",
    )(scal, *queries, *pieces)


def join_kernel(first, second, third, fourth, front_ref, back_ref):
    rows = first.shape[0]
    front_ref[0:rows] = first[...]
    front_ref[rows:] = second[...]
    back_ref[0:rows] = third[...]
    back_ref[rows:] = fourth[...]


def join_call(*parts):
    vmem = pl.BlockSpec(memory_space=pltpu.VMEM)
    rows, width = parts[0].shape
    return pl.pallas_call(
        join_kernel,
        out_shape=(jax.ShapeDtypeStruct((2 * rows, width), BF16),) * 2,
        in_specs=[vmem] * 4,
        out_specs=(vmem, vmem),
        compiler_params=params(),
        cost_estimate=cost(1e9, 2 * MIB),
        name="join",
    )(*parts)


def permute(value, target):
    pairs = []
    for place in range(NY * NX * NCORE):
        y, x, c = place // (NX * NCORE), (place // NCORE) % NX, place % NCORE
        y, x, c = target(y, x, c)
        pairs.append((place, ((y % NY) * NX + x % NX) * NCORE + c))
    return lax.ppermute(value, "seq", pairs)


def swap(value):
    return permute(value, lambda y, x, c: (y, x, 1 - c))


def along(value, step, second):
    def target(y, x, c):
        return (y, x + step, c) if c == second else (y + step, x, c)

    return permute(value, target)


ALL_CHIPS = [[chip * NCORE + core for chip in range(CHIPS)] for core in range(NCORE)]


def exchange(value):
    return lax.all_to_all(value, "seq", 0, 0, axis_index_groups=ALL_CHIPS, tiled=True)


def mirror(value, to_low, first_chip=10):
    seq = CHIPS * NCORE
    pairs = [(place, seq - 1 - place) for place in range(first_chip * NCORE, seq)]
    return lax.ppermute(value, "seq", pairs if to_low else [(low, high) for high, low in pairs])


def local(
    token_ids,
    token_tables,
    ssm_input,
    ssm_gate,
    ssm_bc,
    conv_input,
    conv_bc,
    skip_gain,
    norm_gain,
    queries,
    keys_values,
):
    place = lax.axis_index("seq")
    core = lax.rem(place, NCORE)
    chip = place // NCORE
    keep = core.reshape(1)

    kv = keys_values.reshape(ROWS, 4, HDIM)
    zero = jnp.concatenate([kv[:, 0], kv[:, 2]], 1)
    one = jnp.concatenate([kv[:, 1], kv[:, 3]], 1)
    mine = jnp.where(core == 0, zero, one)
    from_other = swap(jnp.where(core == 0, one, zero))

    bc = ssm_bc.reshape(ROWS, -1)
    edge = jnp.concatenate([ssm_input[ROWS - 16 :], bc[ROWS - 16 :]], 1)
    seq = NY * NX * NCORE
    front = lax.ppermute(edge, "seq", [(i, i + 1) for i in range(seq - 1)])

    scal = jnp.stack([core, chip]).astype(jnp.int32)
    together = lax.optimization_barrier

    query_other = lax.dynamic_slice_in_dim(queries, (1 - core) * HALF, HALF, 1)
    near = swap(query_other)
    far = mirror(query_other, True)
    row, col = table_call(token_ids, token_tables)
    from_other, row, col = together((from_other, row, col))
    unit = jnp.where(
        core == 0,
        jnp.concatenate([mine, from_other], 0),
        jnp.concatenate([from_other, mine], 0),
    )
    left, right, across = (along(unit, step, 0) for step in (1, -1, 2))
    taps_bc = conv_bc.reshape(CONV, -1)
    send = 1 - keep
    x_s, b_s, c_s, state_s = state_call(send, ssm_input, front, conv_input, bc, taps_bc, col)
    state_o = swap(state_s)
    left, right, across, x_s = together((left, right, across, x_s))
    line_a, line_b = join_call(unit, left, right, across)
    left_a, right_b = along(line_a, 1, 1), along(line_b, -1, 1)
    left_b, right_a = along(line_b, 1, 1), along(line_a, -1, 1)
    line_a, line_b, col_k = together((line_a, line_b, col))
    x_k, b_k, c_k, state_k = state_call(keep, ssm_input, front, conv_input, bc, taps_bc, col_k)
    joined = combine_call(keep, state_k, state_o)
    joined, x_s, x_k = together((joined, x_s, x_k))
    arrived = exchange(joined)
    left_a, right_b, left_b, right_a, near, far, x_s = together(
        (left_a, right_b, left_b, right_a, near, far, x_s)
    )
    across_a, across_b = along(left_a, 1, 1), along(right_b, -1, 1)
    y_s = inside_call(send, x_s, b_s, c_s, row, col, skip_gain)
    y_k = inside_call(keep, x_k, b_k, c_k, row, col, skip_gain)
    pieces = [line_a, line_b, left_a, left_b, right_a, right_b, across_a, across_b]
    arrived, y_k, y_s, state_k = together((arrived, y_k, y_s, state_k))
    first_s = swap(state_k)
    before = prefix_call(arrived)
    entering_k = exchange(before)
    scal, before = together((scal, before))
    own, near_out, far_out = attention_call(
        scal, ("own", "near", "far"), [queries, near, far], pieces
    )
    y_k, y_s, far_out, near_out, entering_k = together((y_k, y_s, far_out, near_out, entering_k))
    entering_s = swap(entering_k)
    back_b = mirror(far_out[:, SHARE_LANES:], False)
    back_a = mirror(far_out[:, :SHARE_LANES], False, 14)
    near_back = swap(near_out)

    gain = norm_gain.reshape(1, -1)
    place_k = jnp.stack([core, core]).astype(jnp.int32)
    place_s = jnp.stack([1 - core, core]).astype(jnp.int32)
    mixed = output_call(place_k, entering_k, state_o, c_k, col, y_k, ssm_gate, gain, None)
    mixed = output_call(place_s, entering_s, first_s, c_s, col, y_s, ssm_gate, gain, mixed)
    give = given(chip)
    mixed, back_a, back_b, near_back = together((mixed, back_a, back_b, near_back))
    other = jnp.concatenate(
        [
            jnp.where(give >= 2, back_a, near_back[:, :SHARE_LANES]),
            jnp.where(give >= 1, back_b, near_back[:, SHARE_LANES:]),
        ],
        1,
    )
    attn = jnp.where(
        core == 0, jnp.concatenate([own, other], 1), jnp.concatenate([other, own], 1)
    )
    return mixed, attn


def solution(mesh):
    in_specs = (
        P(("dp", "seq")),
        P(None, "head", None),
        P(("dp", "seq"), "head"),
        P(("dp", "seq"), "head"),
        P(("dp", "seq"), None, "head"),
        P(None, "head"),
        P(None, None, "head"),
        P("head"),
        P("head"),
        P(("dp", "seq"), "head"),
        P(("dp", "seq"), None, "head"),
    )
    out_specs = (P(("dp", "seq"), "head"), P(("dp", "seq"), "head"))
    return jax.shard_map(local, mesh=mesh, in_specs=in_specs, out_specs=out_specs, check_vma=False)
```
